128 devices in a mesh: region: 32 (over x, y, core), grp: 4 (over z).
Axes of the slice: x: 4, y: 4, z: 4, core: 2. Of those that a mesh axis runs over, the one named last changes fastest.
Arguments:
- ensemble: float32 [80, 16, 65536], P('grp', None, 'region')
- loc_weight: bfloat16 [8, 65536, 256], P(None, ('region', 'grp')), may hold values from 0.019897461 to 0.5
- obs_value: float32 [8, 256], replicated, may hold values from -6 to 6
- obs_var: float32 [8, 256], replicated, may hold values from 0.1 to 1
- owner_region: int32 [8], replicated, may hold values from 0 to 31
- obs_cell: int32 [8, 256], replicated, may hold values from 0 to 32767
- batch_order: int32 [8], replicated, may hold values from 0 to 7, each once
Outputs:
- analysis: float32 [80, 16, 65536], P('grp', None, 'region')
The draws below stay inside these ranges and needn't reach their ends.
Inputs may be any that keep to these rules, and one draw needn't show every extreme that they name: `batch_order`: each batch index appears once.
All inputs are finite; a program needn't handle non-finite values.
Results may differ from the reference program's by a relative error of at most 0.0003.
Values sent between devices are 32-bit elements; how exact they have to be, the bound alone decides.
A program may use at most 128 MiB of HBM per device.

```python
import math
import jax
import jax.numpy as jnp
from jax import lax

MEMBERS = 80
STACK = 16
COLS_REG = 2048
COLS = 65536
OBS = 256
BATCHES = 8
N_REGION = 32


def draw_ensemble(key, part):
    key = jax.random.fold_in(key, 7)
    first, second, third = jax.random.split(key, 3)
    noise = jax.random.normal(first, (MEMBERS, STACK, COLS), jnp.float32)
    scales = jnp.exp(jax.random.uniform(second, (1, STACK, COLS), jnp.float32, math.log(0.3), math.log(3.0)))
    centres = 0.5 * jax.random.normal(third, (1, STACK, COLS), jnp.float32)
    return (centres + scales * noise).astype(jnp.float32)


def plant(entries, own_key, low, top_value):
    extent = entries.shape
    spot = [jax.random.randint(jax.random.fold_in(own_key, axis), (), 0, extent[axis]) for axis in range(len(extent))]
    entries = entries.at[tuple(spot)].set(low)
    longest = extent.index(max(extent))
    spot[longest] = (spot[longest] + 1) % extent[longest]
    return entries.at[tuple(spot)].set(top_value)


def block_levels(rng, shape, pieces, least, largest):
    def one(position, parts):
        steps = jax.random.uniform(jax.random.fold_in(jax.random.fold_in(rng, 6), position), (parts,), jnp.float32, least / len(pieces), largest / len(pieces))
        return jnp.repeat(jnp.exp(steps), shape[position] // parts).reshape((-1,) + (1,) * (len(shape) - position - 1))

    gain = one(*pieces[0])
    for cut in pieces[1:]:
        gain = gain * one(*cut)
    return gain


def centred(rng, shape, deviation, bound, dtype=jnp.bfloat16):
    return jnp.clip(deviation * jax.random.normal(rng, shape, jnp.float32), -bound, bound).astype(dtype)


def setup_inputs(seed: int = 0) -> dict:
    seeds = jax.random.split(jax.random.key(seed), 8)
    return {
        "ensemble": draw_ensemble(jax.random.fold_in(seeds[7], 71), 0),
        "loc_weight": jnp.clip(jnp.exp(math.log(0.5) - 3.224016 * jax.random.uniform(seeds[1], (BATCHES, COLS, OBS), jnp.float32) ** block_levels(seeds[1], (BATCHES, COLS, OBS), ((1, 128),), -0.2, 0.2)), 0.019897461, 0.5).astype(jnp.bfloat16),
        "obs_value": centred(seeds[2], (BATCHES, OBS), 1.0, 6.0, jnp.float32),
        "obs_var": jnp.clip(jnp.exp(jax.random.uniform(seeds[3], (BATCHES, OBS), jnp.float32, math.log(0.1), math.log(1.0))), 0.1, 1.0),
        "owner_region": plant(jax.random.randint(seeds[4], (BATCHES,), 0, N_REGION), jax.random.fold_in(seeds[4], 1), 0, N_REGION - 1).astype(jnp.int32),
        "obs_cell": plant(jax.random.randint(seeds[5], (BATCHES, OBS), 0, STACK * COLS_REG), jax.random.fold_in(seeds[5], 1), 0, (STACK * COLS_REG) - 1).astype(jnp.int32),
        "batch_order": jax.random.permutation(seeds[6], BATCHES).astype(jnp.int32),
    }


epsilon = 1e-05

def statistics(prior_obs):
    members = prior_obs.shape[0]
    centre = lax.optimization_barrier(jnp.mean(prior_obs, 0))
    obs_anom = prior_obs - centre
    spread = lax.optimization_barrier(jnp.sum(obs_anom * obs_anom, 0)) / (members - 1) + epsilon
    return (centre, obs_anom, spread)

def adjust(prior_obs, centre, obs_anom, spread, values, variance):
    denom_sum = spread + variance
    post_centre = (variance * centre + spread * values) / denom_sum
    factor = jnp.sqrt(variance / denom_sum)
    return post_centre + factor * obs_anom - prior_obs

def regress(state_blk, weights_blk, obs_anom, change, spread):
    members = state_blk.shape[0]
    width = weights_blk.shape[0]
    centre = lax.optimization_barrier(jnp.mean(state_blk, 0))
    state_anom = (state_blk - centre).reshape(members, -1)
    covariance = lax.dot_general(state_anom, obs_anom, (((0,), (0,)), ((), ())), precision=lax.Precision.HIGHEST)
    inverse_var = 1.0 / ((members - 1) * spread)
    kalman_gain = covariance.reshape(-1, width, obs_anom.shape[1]) * weights_blk.astype(jnp.float32)[None] * inverse_var
    kalman_gain = kalman_gain.reshape(-1, obs_anom.shape[1])
    increment = lax.dot_general(change, kalman_gain, (((1,), (1,)), ((), ())), precision=lax.Precision.HIGHEST)
    return state_blk + increment.reshape(state_blk.shape)

def reference(ensemble, loc_weight, obs_value, obs_var, owner_region, obs_cell, batch_order):
    state = ensemble
    for turn in range(BATCHES):
        batch = batch_order[turn]
        region_id = owner_region[batch]
        cell_ids = obs_cell[batch]
        level_idx = (cell_ids // COLS_REG).astype(jnp.int32)
        column_idx = (region_id * COLS_REG + cell_ids % COLS_REG).astype(jnp.int32)
        prior_obs = state[:, level_idx, column_idx]
        centre, obs_anom, spread = statistics(prior_obs)
        change = adjust(prior_obs, centre, obs_anom, spread, obs_value[batch], obs_var[batch])
        blocks = state.reshape(MEMBERS, STACK, N_REGION, COLS_REG).transpose(2, 0, 1, 3)
        weights = loc_weight[batch].reshape(N_REGION, COLS_REG, OBS)

        def update_block(block_args):
            return regress(block_args[0], block_args[1], obs_anom, change, spread)
        updated = lax.map(update_block, (blocks, weights))
        state = updated.transpose(1, 2, 0, 3).reshape(MEMBERS, STACK, COLS)
    return state
```

```python
import functools

import jax
import jax.numpy as jnp
from jax import lax
from jax.experimental import pallas as pl
from jax.experimental.pallas import tpu as pltpu
from jax.sharding import PartitionSpec as P

epsilon = 1e-05
MESH = pl.DeviceIdType.MESH
F32, BF16 = jnp.float32, jnp.bfloat16

TURNS, OBS, MEM, SLAB, STACK = 8, 256, 80, 20, 16
COLS_REG, COLS_DEV = 2048, 512
GROUP = 4
PAIRS = [(a, b) for h in (0, GROUP) for b in range(h, h + GROUP) for a in range(h, b)]
PAIR_ROW = {p: i * OBS for i, p in enumerate(PAIRS)}
CROSS = [(a, b) for b in range(GROUP, TURNS) for a in range(GROUP)]
CROSS_AT = {p: i for i, p in enumerate(CROSS)}
X0_ROW = len(PAIRS) * OBS
A_ROWS = 3840
D_ROWS = 384
CHUNKS, CHUNK = 4, 128
WIDE = 4


def split2(value):
    high = value.astype(BF16)
    low = (value - high.astype(F32)).astype(BF16)
    return high, low


def increment(x, left, change, weights):
    anom = x - jnp.sum(x, 0, keepdims=True) * (1.0 / MEM)
    high, low = split2(anom)
    stacked = jnp.concatenate([high, high, low], 0)
    gain = jnp.dot(left, stacked, preferred_element_type=F32) * weights
    g_high, g_low = split2(gain)
    first = jnp.dot(change, g_high, preferred_element_type=F32)
    second = jnp.dot(change[:MEM], g_low, preferred_element_type=F32)
    return first[:MEM] + first[MEM:] + second


def turn_operands(prior, value, variance):
    centre = jnp.sum(prior, 0, keepdims=True) * (1.0 / MEM)
    anom = prior - centre
    spread = jnp.sum(anom * anom, 0, keepdims=True) / (MEM - 1) + epsilon
    denom = spread + variance
    post = (variance * centre + spread * value) / denom
    factor = jnp.sqrt(variance / denom)
    change = post + factor * anom - prior
    scaled = anom * (1.0 / ((MEM - 1) * spread))
    high = scaled.astype(BF16).astype(F32)
    low = scaled - high
    left = jnp.concatenate([high, low, high], 0).T.astype(BF16)
    c_high, c_low = split2(change)
    return left, jnp.concatenate([c_high, c_low], 0)


def pick_kernel(order, owner, cells, ens, out, held, sem):
    here = lax.axis_index("region")
    out[...] = jnp.zeros_like(out)
    mine = [owner[order[t]] == here for t in range(TURNS)]
    some = functools.reduce(jnp.logical_or, mine)

    @pl.when(some)
    def _():
        copy = pltpu.make_async_copy(ens, held, sem)
        copy.start()
        copy.wait()

    for t in range(TURNS):

        @pl.when(mine[t])
        def _(t=t):
            cell = cells[pl.ds(order[t], 1), :]
            column = cell & (COLS_REG - 1)
            level = cell >> 11
            depth = 512

            def part(k, total):
                at = pl.multiple_of(k * depth, depth)
                rows = lax.broadcasted_iota(jnp.int32, (depth, OBS), 0) + at
                select = jnp.where(rows == column, 1.0, 0.0).astype(BF16)
                value = held[:, pl.ds(at, depth)]
                high = value.astype(BF16)
                rest = value - high.astype(F32)
                middle, low = split2(rest)
                for piece in (high, middle, low):
                    total = total + jnp.dot(piece, select, preferred_element_type=F32)
                return total

            total = lax.fori_loop(0, COLS_REG // depth, part, jnp.zeros((SLAB * STACK, OBS), F32))
            total = total.reshape(SLAB, STACK, OBS)
            levels = lax.broadcasted_iota(jnp.int32, (SLAB, STACK, OBS), 1)
            out[t, 0:SLAB, :] = jnp.sum(jnp.where(levels == level[None], total, 0.0), 1)


def places():
    region, z = lax.axis_index("region"), lax.axis_index("grp")
    return region // 8, (region // 2) % 4, region % 2, z


def peer(axis, k):
    x, y, c, z = places()
    if axis == "x":
        x = lax.rem(x + k, 4)
    elif axis == "y":
        y = lax.rem(y + k, 4)
    elif axis == "z":
        z = lax.rem(z + k, 4)
    else:
        c = 1 - c
    return (x * 8 + y * 2 + c, z)


def all_reduce(a, b, rows, sib, inbox, sib_sem, send, recv):
    x, y, c, z = places()
    at = {"x": x, "y": y, "z": z}
    axes = ("x", "y", "z")
    q = rows // 24
    t, h = 4 * q, 12 * q
    base, other = pl.multiple_of(c * h, 8), pl.multiple_of((1 - c) * h, 8)
    own = [pl.multiple_of(base + i * t + at[axes[i]] * q, 8) for i in range(3)]

    def remote(src, dst, s, r, device):
        return pltpu.make_async_remote_copy(src, dst, s, r, device_id=device, device_id_type=MESH)

    copy = remote(a.at[pl.ds(other, h)], sib, sib_sem.at[0], sib_sem.at[1], peer("c", 1))
    copy.start()
    copy.wait()
    a[pl.ds(base, h), :] += sib[...]
    for phase in range(3):
        copies = []
        for k in (1, 2, 3):
            for i in range(3):
                axis = axes[(i + phase) % 3]
                if phase == 0:
                    src = pl.multiple_of(base + i * t + lax.rem(at[axis] + k, 4) * q, 8)
                else:
                    src = own[i]
                copy = remote(a.at[pl.ds(src, q)], inbox.at[phase, i, k - 1], send.at[phase, i, k - 1],
                              recv.at[phase, i, k - 1], peer(axis, k))
                copy.start()
                copies.append(copy)
        for copy in copies:
            copy.wait()
        for i in range(3):
            into = b if phase == 2 else a
            into[pl.ds(own[i], q), :] = (
                a[pl.ds(own[i], q), :] + inbox[phase, i, 0] + inbox[phase, i, 1] + inbox[phase, i, 2])
    copies = []
    for k in (1, 2, 3):
        for i in range(3):
            rows_i = b.at[pl.ds(own[i], q)]
            copy = remote(rows_i, rows_i, send.at[3, i, k - 1], recv.at[3, i, k - 1], peer(axes[i], k))
            copy.start()
            copies.append(copy)
    for copy in copies:
        copy.wait()
    half = b.at[pl.ds(base, h)]
    copy = remote(half, half, sib_sem.at[2], sib_sem.at[3], peer("c", 1))
    copy.start()
    copy.wait()


def main_kernel(order, owner, cells, values, variances, weights, picked, ens, out,
                stage, outbox, a, a_sum, d, d_sum, wt, cross, prior, left, change, tile,
                sib_a, in_a, sib_d, in_d,
                go_send, go_recv, go_own, back_send, back_recv, back_own,
                sibsem_a, send_a, recv_a, sibsem_d, send_d, recv_d):
    region, z = lax.axis_index("region"), lax.axis_index("grp")

    barrier = pltpu.get_barrier_semaphore()
    around = [peer(axis, k) for axis in ("x", "y", "z") for k in (1, 2, 3)] + [peer("c", 1)]
    for device in around:
        pl.semaphore_signal(barrier, 1, device_id=device, device_id_type=MESH)
    pl.semaphore_wait(barrier, len(around))

    go = []
    for k in (1, 2, 3):
        to = lax.rem(z + k, 4)
        for q in range(CHUNKS):
            src = ens.at[:, pl.ds(pl.multiple_of(to * COLS_DEV + q * CHUNK, 128), CHUNK)]
            go.append(pltpu.make_async_remote_copy(
                src, stage.at[z, q], go_send.at[q, k - 1], go_recv.at[q, k - 1],
                device_id=peer("z", k), device_id_type=MESH))
    for q in range(CHUNKS):
        src = ens.at[:, pl.ds(pl.multiple_of(z * COLS_DEV + q * CHUNK, 128), CHUNK)]
        go.append(pltpu.make_async_copy(src, stage.at[z, q], go_own.at[q]))
    for copy in go:
        copy.start()

    for t in range(TURNS):
        wt[t] = weights[order[t]].astype(F32).T.astype(BF16)

    for b in range(TURNS):
        column = cells[pl.ds(order[b], 1), :] & (COLS_REG - 1)
        local = column - z * COLS_DEV
        local = jnp.where(owner[order[b]] == region, local, -1)
        select = jnp.where(lax.broadcasted_iota(jnp.int32, (COLS_DEV, OBS), 0) == local, 1.0, 0.0).astype(BF16)
        for t in range(b):
            rows = jnp.dot(wt[t], select, preferred_element_type=F32)
            if (t, b) in PAIR_ROW:
                a[PAIR_ROW[t, b]:PAIR_ROW[t, b] + OBS, :] = rows
            else:
                cross[CROSS_AT[t, b]] = rows.astype(BF16)
        for k in range(4):
            at = X0_ROW + b * MEM + k * SLAB
            a[at:at + SLAB, :] = jnp.where(z == k, picked[b, 0:SLAB, :], 0.0)
    a[X0_ROW + TURNS * MEM:A_ROWS, :] = jnp.zeros((A_ROWS - X0_ROW - TURNS * MEM, OBS), F32)
    d[...] = jnp.zeros_like(d)

    all_reduce(a, a_sum, A_ROWS, sib_a, in_a, sibsem_a, send_a, recv_a)

    for t in range(TURNS):
        prior[t] = a_sum[X0_ROW + t * MEM:X0_ROW + (t + 1) * MEM, :]

    for t in range(TURNS):
        if t == GROUP:
            all_reduce(d, d_sum, D_ROWS, sib_d, in_d, sibsem_d, send_d, recv_d)
            for b in range(GROUP, TURNS):
                at = (b - GROUP) * MEM
                prior[b] = a_sum[X0_ROW + b * MEM:X0_ROW + (b + 1) * MEM, :] + d_sum[at:at + MEM, :]
        left[t], change[t] = turn_operands(
            prior[t], values[pl.ds(order[t], 1), :], variances[pl.ds(order[t], 1), :])
        for b in range(t + 1, TURNS):
            if (t, b) in PAIR_ROW:
                row = PAIR_ROW[t, b]
                prior[b] += increment(prior[b], left[t], change[t], a_sum[row:row + OBS, :])
            else:
                at = (b - GROUP) * MEM
                step = increment(prior[b], left[t], change[t], cross[CROSS_AT[t, b]].astype(F32))
                d[at:at + MEM, :] += step
                prior[b] += step

    for copy in go:
        copy.wait()

    def send_back(q):
        there = pl.ds(pl.multiple_of(z * COLS_DEV + q * CHUNK, 128), CHUNK)
        for k in (1, 2, 3):
            to = lax.rem(z + k, 4)
            yield pltpu.make_async_remote_copy(
                outbox.at[to, q], out.at[:, there], back_send.at[q, k - 1], back_recv.at[q, k - 1],
                device_id=peer("z", k), device_id_type=MESH)
        yield pltpu.make_async_copy(outbox.at[z, q], out.at[:, there], back_own.at[q])

    def chunk(q, _):
        lanes = pl.ds(pl.multiple_of(q * CHUNK, 128), CHUNK)

        def levels(sg, _):
            for w in range(WIDE):
                for k in range(4):
                    tile[k * SLAB:(k + 1) * SLAB, w * CHUNK:(w + 1) * CHUNK] = stage[
                        k, q, pl.ds(sg * WIDE + w, SLAB, stride=STACK), :]

            def turn(t, _):
                w_t = wt[t, :, lanes].astype(F32)
                w_t = jnp.concatenate([w_t] * WIDE, 1)
                x = tile[...]
                tile[...] = x + increment(x, left[t], change[t], w_t)
                return 0

            lax.fori_loop(0, TURNS, turn, 0)
            for w in range(WIDE):
                for k in range(4):
                    outbox[k, q, pl.ds(sg * WIDE + w, SLAB, stride=STACK), :] = tile[
                        k * SLAB:(k + 1) * SLAB, w * CHUNK:(w + 1) * CHUNK]
            return 0

        lax.fori_loop(0, STACK // WIDE, levels, 0)
        for copy in send_back(q):
            copy.start()
        return 0

    lax.fori_loop(0, CHUNKS, chunk, 0)
    for q in range(CHUNKS):
        for copy in send_back(q):
            copy.wait()


def body(ensemble, loc_weight, obs_value, obs_var, owner_region, obs_cell, batch_order):
    flat = ensemble.reshape(SLAB * STACK, COLS_REG)
    smem, vmem, anywhere = (pl.BlockSpec(memory_space=m) for m in (pltpu.SMEM, pltpu.VMEM, pl.ANY))
    picked = pl.pallas_call(
        pick_kernel,
        out_shape=jax.ShapeDtypeStruct((TURNS, 24, OBS), F32),
        in_specs=[smem, smem, vmem, anywhere],
        out_specs=vmem,
        scratch_shapes=[pltpu.VMEM((SLAB * STACK, COLS_REG), F32), pltpu.SemaphoreType.DMA],
        compiler_params=pltpu.CompilerParams(vmem_limit_bytes=48 << 20),
        name="pick",
    )(batch_order, owner_region, obs_cell, flat)

    qa, qd = A_ROWS // 24, D_ROWS // 24
    dma = pltpu.SemaphoreType.DMA
    out = pl.pallas_call(
        main_kernel,
        out_shape=jax.ShapeDtypeStruct((SLAB * STACK, COLS_REG), F32),
        in_specs=[smem, smem, vmem, vmem, vmem, vmem, vmem, anywhere],
        out_specs=anywhere,
        scratch_shapes=[
            pltpu.VMEM((4, CHUNKS, SLAB * STACK, CHUNK), F32),
            pltpu.VMEM((4, CHUNKS, SLAB * STACK, CHUNK), F32),
            pltpu.VMEM((A_ROWS, OBS), F32), pltpu.VMEM((A_ROWS, OBS), F32),
            pltpu.VMEM((D_ROWS, OBS), F32), pltpu.VMEM((D_ROWS, OBS), F32),
            pltpu.VMEM((TURNS, OBS, COLS_DEV), BF16),
            pltpu.VMEM((len(CROSS), OBS, OBS), BF16),
            pltpu.VMEM((TURNS, MEM, OBS), F32),
            pltpu.VMEM((TURNS, OBS, 3 * MEM), BF16),
            pltpu.VMEM((TURNS, 2 * MEM, OBS), BF16),
            pltpu.VMEM((MEM, WIDE * CHUNK), F32),
            pltpu.VMEM((12 * qa, OBS), F32), pltpu.VMEM((3, 3, 3, qa, OBS), F32),
            pltpu.VMEM((12 * qd, OBS), F32), pltpu.VMEM((3, 3, 3, qd, OBS), F32),
            dma((CHUNKS, 3)), dma((CHUNKS, 3)), dma((CHUNKS,)),
            dma((CHUNKS, 3)), dma((CHUNKS, 3)), dma((CHUNKS,)),
            dma((4,)), dma((4, 3, 3)), dma((4, 3, 3)),
            dma((4,)), dma((4, 3, 3)), dma((4, 3, 3)),
        ],
        compiler_params=pltpu.CompilerParams(
            collective_id=0, has_side_effects=True, vmem_limit_bytes=56 << 20),
        name="filter",
    )(batch_order, owner_region, obs_cell, obs_value, obs_var, loc_weight, picked, flat)
    return out.reshape(SLAB, STACK, COLS_REG)


def solution(mesh):
    return jax.shard_map(
        body,
        mesh=mesh,
        in_specs=(P("grp", None, "region"), P(None, ("region", "grp"), None), P(), P(), P(), P(), P()),
        out_specs=P("grp", None, "region"),
        check_vma=False,
    )
```

```python
import functools

import jax
import jax.numpy as jnp
from jax import lax
from jax.experimental import pallas as pl
from jax.experimental.pallas import tpu as pltpu
from jax.sharding import PartitionSpec as P

epsilon = 1e-05
MESH = pl.DeviceIdType.MESH
F32, BF16 = jnp.float32, jnp.bfloat16

TURNS, OBS, MEM, SLAB, STACK = 8, 256, 80, 20, 16
COLS_REG, COLS_DEV = 2048, 512
GROUP = 4
FIRST = [(a, b) for b in range(GROUP) for a in range(b)]
SECOND = [(a, b) for b in range(GROUP, TURNS) for a in range(GROUP, b)]
CROSS = [(a, b) for b in range(GROUP, TURNS) for a in range(GROUP)]
FIRST_ROW = {p: i * OBS for i, p in enumerate(FIRST)}
SECOND_ROW = {p: i * OBS for i, p in enumerate(SECOND)}
CROSS_AT = {p: i for i, p in enumerate(CROSS)}
X0_ROW = len(FIRST) * OBS
A_ROWS = 2560
B_ROWS = len(SECOND) * OBS
D_ROWS = 384
CHUNKS, CHUNK = 4, 128
CELLS = STACK * CHUNK


def split2(value):
    high = value.astype(BF16)
    low = (value - high.astype(F32)).astype(BF16)
    return high, low


def increment(x, left, change, weights):
    anom = x - jnp.sum(x, 0, keepdims=True) * (1.0 / MEM)
    high, low = split2(anom)
    stacked = jnp.concatenate([high, high, low], 0)
    gain = jnp.dot(left, stacked, preferred_element_type=F32) * weights
    g_high, g_low = split2(gain)
    first = jnp.dot(change, g_high, preferred_element_type=F32)
    second = jnp.dot(change[:MEM], g_low, preferred_element_type=F32)
    return first[:MEM] + first[MEM:] + second


def turn_operands(prior, value, variance):
    centre = jnp.sum(prior, 0, keepdims=True) * (1.0 / MEM)
    anom = prior - centre
    spread = jnp.sum(anom * anom, 0, keepdims=True) / (MEM - 1) + epsilon
    denom = spread + variance
    post = (variance * centre + spread * value) / denom
    factor = jnp.sqrt(variance / denom)
    change = post + factor * anom - prior
    scaled = anom * (1.0 / ((MEM - 1) * spread))
    high = scaled.astype(BF16).astype(F32)
    low = scaled - high
    left = jnp.concatenate([high, low, high], 0).T.astype(BF16)
    c_high, c_low = split2(change)
    return left, jnp.concatenate([c_high, c_low], 0)


def pick_kernel(order, owner, cells, ens, out, held, sem):
    here = lax.axis_index("region")
    out[...] = jnp.zeros_like(out)
    mine = [owner[order[t]] == here for t in range(TURNS)]
    some = functools.reduce(jnp.logical_or, mine)

    @pl.when(some)
    def _():
        copy = pltpu.make_async_copy(ens, held, sem)
        copy.start()
        copy.wait()

    for t in range(TURNS):

        @pl.when(mine[t])
        def _(t=t):
            cell = cells[pl.ds(order[t], 1), :]
            column = cell & (COLS_REG - 1)
            level = cell >> 11
            depth = 512

            def part(k, total):
                at = pl.multiple_of(k * depth, depth)
                rows = lax.broadcasted_iota(jnp.int32, (depth, OBS), 0) + at
                select = jnp.where(rows == column, 1.0, 0.0).astype(BF16)
                value = held[:, pl.ds(at, depth)]
                high = value.astype(BF16)
                rest = value - high.astype(F32)
                middle, low = split2(rest)
                for piece in (high, middle, low):
                    total = total + jnp.dot(piece, select, preferred_element_type=F32)
                return total

            total = lax.fori_loop(0, COLS_REG // depth, part, jnp.zeros((SLAB * STACK, OBS), F32))
            total = total.reshape(SLAB, STACK, OBS)
            levels = lax.broadcasted_iota(jnp.int32, (SLAB, STACK, OBS), 1)
            out[t, 0:SLAB, :] = jnp.sum(jnp.where(levels == level[None], total, 0.0), 1)


def places():
    region, z = lax.axis_index("region"), lax.axis_index("grp")
    return region // 8, (region // 2) % 4, region % 2, z


def peer(axis, k):
    x, y, c, z = places()
    if axis == "x":
        x = lax.rem(x + k, 4)
    elif axis == "y":
        y = lax.rem(y + k, 4)
    elif axis == "z":
        z = lax.rem(z + k, 4)
    else:
        c = 1 - c
    return (x * 8 + y * 2 + c, z)


def remote(src, dst, send, recv, device):
    return pltpu.make_async_remote_copy(src, dst, send, recv, device_id=device, device_id_type=MESH)


def started(copies):
    for copy in copies:
        copy.start()
    return copies


def wait(copies):
    for copy in copies:
        copy.wait()


def swap_halves(src, dst, sems, k):
    return started([remote(src, dst, sems.at[2 * k], sems.at[2 * k + 1], peer("c", 1))])


def small_sum(a, b, rows, sib, inbox, sib_sem, send, recv):
    x, y, c, z = places()
    at = {"x": x, "y": y, "z": z}
    axes = ("x", "y", "z")
    q = rows // 24
    t, h = 4 * q, 12 * q
    base, other = pl.multiple_of(c * h, 8), pl.multiple_of((1 - c) * h, 8)
    own = [pl.multiple_of(base + i * t + at[axes[i]] * q, 8) for i in range(3)]

    copies = swap_halves(a.at[pl.ds(other, h)], sib, sib_sem, 0)
    yield
    wait(copies)
    a[pl.ds(base, h), :] += sib[...]
    for phase in range(3):
        copies = []
        for k in (1, 2, 3):
            for i in range(3):
                axis = axes[(i + phase) % 3]
                src = own[i]
                if phase == 0:
                    src = pl.multiple_of(base + i * t + lax.rem(at[axis] + k, 4) * q, 8)
                copies.append(remote(a.at[pl.ds(src, q)], inbox.at[phase, i, k - 1], send.at[phase, i, k - 1],
                                     recv.at[phase, i, k - 1], peer(axis, k)))
        started(copies)
        yield
        wait(copies)
        for i in range(3):
            into = b if phase == 2 else a
            into[pl.ds(own[i], q), :] = (
                a[pl.ds(own[i], q), :] + inbox[phase, i, 0] + inbox[phase, i, 1] + inbox[phase, i, 2])
    copies = []
    for k in (1, 2, 3):
        for i in range(3):
            rows_i = b.at[pl.ds(own[i], q)]
            copies.append(remote(rows_i, rows_i, send.at[3, i, k - 1], recv.at[3, i, k - 1], peer(axes[i], k)))
    started(copies)
    yield
    wait(copies)
    half = b.at[pl.ds(base, h)]
    copies = swap_halves(half, half, sib_sem, 1)
    yield
    wait(copies)


def big_sum(a, b, rows, sib, in0, in1, in2, sib_sem, send, recv):
    x, y, c, z = places()
    at = {"x": x, "y": y}
    orders = (("x", "y"), ("y", "x"))
    h = rows // 2
    t = h // 2
    q, r = t // 4, t // 16
    base, other = pl.multiple_of(c * h, 8), pl.multiple_of((1 - c) * h, 8)
    block = [pl.multiple_of(base + i * t, 8) for i in range(2)]
    quarter = [pl.multiple_of(block[i] + at[orders[i][0]] * q, 8) for i in range(2)]
    own = [pl.multiple_of(quarter[i] + at[orders[i][1]] * r, 8) for i in range(2)]

    copies = swap_halves(a.at[pl.ds(other, h)], sib, sib_sem, 0)
    yield
    wait(copies)
    a[pl.ds(base, h), :] += sib[...]

    def exchange(phase, pick, inbox, axis_of):
        return started([
            remote(a.at[pl.ds(pick(i, k), inbox.shape[2])], inbox.at[i, k - 1], send.at[phase, i, k - 1],
                   recv.at[phase, i, k - 1], peer(axis_of(i), k))
            for k in (1, 2, 3) for i in range(2)])

    def added(i, at, inbox):
        return a[pl.ds(at, inbox.shape[2]), :] + inbox[i, 0] + inbox[i, 1] + inbox[i, 2]

    copies = exchange(0, lambda i, k: pl.multiple_of(block[i] + lax.rem(at[orders[i][0]] + k, 4) * q, 8),
                      in0, lambda i: orders[i][0])
    yield
    wait(copies)
    for i in range(2):
        a[pl.ds(quarter[i], q), :] = added(i, quarter[i], in0)
    copies = exchange(1, lambda i, k: pl.multiple_of(quarter[i] + lax.rem(at[orders[i][1]] + k, 4) * r, 8),
                      in1, lambda i: orders[i][1])
    yield
    wait(copies)
    for i in range(2):
        a[pl.ds(own[i], r), :] = added(i, own[i], in1)
    copies = exchange(2, lambda i, k: own[i], in2, lambda i: "z")
    yield
    wait(copies)
    for i in range(2):
        b[pl.ds(own[i], r), :] = added(i, own[i], in2)

    def gather(phase, place, size, axis_of):
        return started([
            remote(b.at[pl.ds(place[i], size)], b.at[pl.ds(place[i], size)], send.at[phase, i, k - 1],
                   recv.at[phase, i, k - 1], peer(axis_of(i), k))
            for k in (1, 2, 3) for i in range(2)])

    copies = gather(3, own, r, lambda i: orders[i][1])
    yield
    wait(copies)
    copies = gather(4, quarter, q, lambda i: orders[i][0])
    yield
    wait(copies)
    half = b.at[pl.ds(base, h)]
    copies = swap_halves(half, half, sib_sem, 1)
    yield
    wait(copies)


def main_kernel(order, owner, cells, values, variances, weights, picked, ens, out,
                stage, outbox, state, wt, cross, prior, left, change,
                a, a_sum, b, b_sum, d, d_sum, *rest):
    (sib_a, in0_a, in1_a, in2_a, sib_b, in0_b, in1_b, in2_b, sib_d, in_d,
     go_send, go_recv, go_own, back_send, back_recv, back_own,
     sibsem_a, send_a, recv_a, sibsem_b, send_b, recv_b, sibsem_d, send_d, recv_d) = rest
    region, z = lax.axis_index("region"), lax.axis_index("grp")

    barrier = pltpu.get_barrier_semaphore()
    around = [peer(axis, k) for axis in ("x", "y", "z") for k in (1, 2, 3)] + [peer("c", 1)]
    for device in around:
        pl.semaphore_signal(barrier, 1, device_id=device, device_id_type=MESH)
    pl.semaphore_wait(barrier, len(around))

    def go(q):
        here = pl.ds(pl.multiple_of(z * COLS_DEV + q * CHUNK, 128), CHUNK)
        copies = [pltpu.make_async_copy(ens.at[:, here], stage.at[z, q], go_own.at[q])]
        for k in (1, 2, 3):
            there = pl.ds(pl.multiple_of(lax.rem(z + k, 4) * COLS_DEV + q * CHUNK, 128), CHUNK)
            copies.append(remote(ens.at[:, there], stage.at[z, q], go_send.at[q, k - 1], go_recv.at[q, k - 1],
                                 peer("z", k)))
        return started(copies)

    def back(q):
        there = pl.ds(pl.multiple_of(z * COLS_DEV + q * CHUNK, 128), CHUNK)
        copies = [pltpu.make_async_copy(outbox.at[z, q], out.at[:, there], back_own.at[q])]
        for k in (1, 2, 3):
            copies.append(remote(outbox.at[lax.rem(z + k, 4), q], out.at[:, there],
                                 back_send.at[q, k - 1], back_recv.at[q, k - 1], peer("z", k)))
        return copies

    def turned(t):
        wt[t] = weights[order[t]].astype(F32).T.astype(BF16)

    def select(n):
        column = cells[pl.ds(order[n], 1), :] & (COLS_REG - 1)
        local = jnp.where(owner[order[n]] == region, column - z * COLS_DEV, -1)
        return jnp.where(lax.broadcasted_iota(jnp.int32, (COLS_DEV, OBS), 0) == local, 1.0, 0.0).astype(BF16)

    def at_columns(t, chosen):
        return jnp.dot(wt[t], chosen, preferred_element_type=F32)

    sent = go(0) + go(1)
    for t in range(GROUP - 1):
        turned(t)
    for n in range(TURNS):
        if 0 < n < GROUP:
            chosen = select(n)
            for t in range(n):
                row = FIRST_ROW[t, n]
                a[row:row + OBS, :] = at_columns(t, chosen)
        for k in range(4):
            at = X0_ROW + n * MEM + k * SLAB
            a[at:at + SLAB, :] = jnp.where(z == k, picked[n, 0:SLAB, :], 0.0)
    a[X0_ROW + TURNS * MEM:A_ROWS, :] = jnp.zeros((A_ROWS - X0_ROW - TURNS * MEM, OBS), F32)

    sum_a = big_sum(a, a_sum, A_ROWS, sib_a, in0_a, in1_a, in2_a, sibsem_a, send_a, recv_a)
    sum_b = big_sum(b, b_sum, B_ROWS, sib_b, in0_b, in1_b, in2_b, sibsem_b, send_b, recv_b)
    sum_d = small_sum(d, d_sum, D_ROWS, sib_d, in_d, sibsem_d, send_d, recv_d)

    next(sum_a)
    for t in range(GROUP - 1, TURNS):
        turned(t)
    next(sum_a)
    for n in range(GROUP, TURNS):
        chosen = select(n)
        for t in range(n):
            rows = at_columns(t, chosen)
            if t < GROUP:
                cross[CROSS_AT[t, n]] = rows.astype(BF16)
            else:
                row = SECOND_ROW[t, n]
                b[row:row + OBS, :] = rows
    d[...] = jnp.zeros_like(d)
    next(sum_b)
    next(sum_a)
    next(sum_a)
    next(sum_b)
    next(sum_a)
    next(sum_b)
    sent += go(2) + go(3)
    next(sum_a)
    next(sum_b)
    next(sum_a)
    next(sum_a, None)

    def assimilate(t):
        left[t], change[t] = turn_operands(
            prior[t], values[pl.ds(order[t], 1), :], variances[pl.ds(order[t], 1), :])

    for n in range(TURNS):
        prior[n] = a_sum[X0_ROW + n * MEM:X0_ROW + (n + 1) * MEM, :]
    for t in range(GROUP):
        assimilate(t)
        for n in range(t + 1, TURNS):
            if n < GROUP:
                row = FIRST_ROW[t, n]
                prior[n] += increment(prior[n], left[t], change[t], a_sum[row:row + OBS, :])
            else:
                at = (n - GROUP) * MEM
                step = increment(prior[n], left[t], change[t], cross[CROSS_AT[t, n]].astype(F32))
                d[at:at + MEM, :] += step
                prior[n] += step
    next(sum_d)
    next(sum_b)

    def turns(q, first, last):
        lanes = pl.ds(pl.multiple_of(q * CHUNK, 128), CHUNK)

        def turn(t, _):
            w_t = jnp.concatenate([wt[t, :, lanes].astype(F32)] * STACK, 1)
            x = state[q]
            state[q] = x + increment(x, left[t], change[t], w_t)
            return 0

        lax.fori_loop(first, last, turn, 0)

    def early(q):
        def level(s, _):
            lanes = pl.ds(pl.multiple_of(s * CHUNK, 128), CHUNK)
            for k in range(4):
                state[q, k * SLAB:(k + 1) * SLAB, lanes] = stage[k, q, pl.ds(s, SLAB, stride=STACK), :]
            return 0

        lax.fori_loop(0, STACK, level, 0)
        turns(q, 0, GROUP)

    next(sum_d)
    wait(sent)
    early(0)
    next(sum_d)
    next(sum_b)
    early(1)
    next(sum_d)
    next(sum_b)
    early(2)
    next(sum_d)
    next(sum_b, None)
    early(3)
    next(sum_d)
    next(sum_d, None)

    for n in range(GROUP, TURNS):
        at = (n - GROUP) * MEM
        prior[n] = a_sum[X0_ROW + n * MEM:X0_ROW + (n + 1) * MEM, :] + d_sum[at:at + MEM, :]
    for t in range(GROUP, TURNS):
        assimilate(t)
        for n in range(t + 1, TURNS):
            row = SECOND_ROW[t, n]
            prior[n] += increment(prior[n], left[t], change[t], b_sum[row:row + OBS, :])

    def late(q, _):
        turns(q, GROUP, TURNS)

        def level(s, _):
            lanes = pl.ds(pl.multiple_of(s * CHUNK, 128), CHUNK)
            for k in range(4):
                outbox[k, q, pl.ds(s, SLAB, stride=STACK), :] = state[q, k * SLAB:(k + 1) * SLAB, lanes]
            return 0

        lax.fori_loop(0, STACK, level, 0)
        started(back(q))
        return 0

    lax.fori_loop(0, CHUNKS, late, 0)
    for q in range(CHUNKS):
        wait(back(q))


def body(ensemble, loc_weight, obs_value, obs_var, owner_region, obs_cell, batch_order):
    flat = ensemble.reshape(SLAB * STACK, COLS_REG)
    smem, vmem, anywhere = (pl.BlockSpec(memory_space=m) for m in (pltpu.SMEM, pltpu.VMEM, pl.ANY))
    picked = pl.pallas_call(
        pick_kernel,
        out_shape=jax.ShapeDtypeStruct((TURNS, 24, OBS), F32),
        in_specs=[smem, smem, vmem, anywhere],
        out_specs=vmem,
        scratch_shapes=[pltpu.VMEM((SLAB * STACK, COLS_REG), F32), pltpu.SemaphoreType.DMA],
        compiler_params=pltpu.CompilerParams(vmem_limit_bytes=60 << 20),
        name="pick",
    )(batch_order, owner_region, obs_cell, flat)

    dma = pltpu.SemaphoreType.DMA

    def big_room(rows):
        return [pltpu.VMEM((rows // 2, OBS), F32)] + [
            pltpu.VMEM((2, 3, rows // cut, OBS), F32) for cut in (16, 64, 64)]

    out = pl.pallas_call(
        main_kernel,
        out_shape=jax.ShapeDtypeStruct((SLAB * STACK, COLS_REG), F32),
        in_specs=[smem, smem, vmem, vmem, vmem, vmem, vmem, anywhere],
        out_specs=anywhere,
        scratch_shapes=[
            pltpu.VMEM((4, CHUNKS, SLAB * STACK, CHUNK), F32),
            pltpu.VMEM((4, CHUNKS, SLAB * STACK, CHUNK), F32),
            pltpu.VMEM((CHUNKS, MEM, CELLS), F32),
            pltpu.VMEM((TURNS, OBS, COLS_DEV), BF16),
            pltpu.VMEM((len(CROSS), OBS, OBS), BF16),
            pltpu.VMEM((TURNS, MEM, OBS), F32),
            pltpu.VMEM((TURNS, OBS, 3 * MEM), BF16),
            pltpu.VMEM((TURNS, 2 * MEM, OBS), BF16),
            pltpu.VMEM((A_ROWS, OBS), F32), pltpu.VMEM((A_ROWS, OBS), F32),
            pltpu.VMEM((B_ROWS, OBS), F32), pltpu.VMEM((B_ROWS, OBS), F32),
            pltpu.VMEM((D_ROWS, OBS), F32), pltpu.VMEM((D_ROWS, OBS), F32),
            *big_room(A_ROWS), *big_room(B_ROWS),
            pltpu.VMEM((D_ROWS // 2, OBS), F32), pltpu.VMEM((3, 3, 3, D_ROWS // 24, OBS), F32),
            dma((CHUNKS, 3)), dma((CHUNKS, 3)), dma((CHUNKS,)),
            dma((CHUNKS, 3)), dma((CHUNKS, 3)), dma((CHUNKS,)),
            dma((4,)), dma((5, 2, 3)), dma((5, 2, 3)),
            dma((4,)), dma((5, 2, 3)), dma((5, 2, 3)),
            dma((4,)), dma((4, 3, 3)), dma((4, 3, 3)),
        ],
        compiler_params=pltpu.CompilerParams(
            collective_id=0, has_side_effects=True, vmem_limit_bytes=60 << 20),
        name="filter",
    )(batch_order, owner_region, obs_cell, obs_value, obs_var, loc_weight, picked, flat)
    return out.reshape(SLAB, STACK, COLS_REG)


def solution(mesh):
    return jax.shard_map(
        body,
        mesh=mesh,
        in_specs=(P("grp", None, "region"), P(None, ("region", "grp"), None), P(), P(), P(), P(), P()),
        out_specs=P("grp", None, "region"),
        check_vma=False,
    )
```

```python
import functools

import jax
import jax.numpy as jnp
from jax import lax
from jax.experimental import pallas as pl
from jax.experimental.pallas import tpu as pltpu
from jax.sharding import PartitionSpec as P

epsilon = 1e-05
MESH = pl.DeviceIdType.MESH
F32, BF16 = jnp.float32, jnp.bfloat16

TURNS, OBS, MEM, SLAB, STACK = 8, 256, 80, 20, 16
COLS_REG, COLS_DEV = 2048, 512
GROUP = 4
LANES = 128
FIRST = [(a, b) for b in range(GROUP) for a in range(b)]
SECOND = [(a, b) for b in range(GROUP, TURNS) for a in range(GROUP, b)]
CROSS = [(a, b) for b in range(GROUP, TURNS) for a in range(GROUP)]
FIRST_ROW = {p: i * OBS for i, p in enumerate(FIRST)}
SECOND_ROW = {p: i * OBS for i, p in enumerate(SECOND)}
CROSS_AT = {p: i for i, p in enumerate(CROSS)}
A_ROWS = 2 * len(FIRST) * OBS
B_ROWS = 2 * len(SECOND) * OBS
D_USED = 2 * (TURNS - GROUP) * MEM
D_ROWS = -(-D_USED // 128) * 128
X_ROWS = TURNS * 24 // 2
CHUNKS, CHUNK = 4, 128
CELLS = STACK * CHUNK
EARLY = [GROUP, GROUP - 1, GROUP - 1, GROUP - 1]


def split2(value):
    high = value.astype(BF16)
    low = (value - high.astype(F32)).astype(BF16)
    return high, low


def increment(x, left, change, weights):
    anom = x - jnp.sum(x, 0, keepdims=True) * (1.0 / MEM)
    high, low = split2(anom)
    stacked = jnp.concatenate([high, high, low], 0)
    gain = jnp.dot(left, stacked, preferred_element_type=F32) * weights
    g_high, g_low = split2(gain)
    first = jnp.dot(change, g_high, preferred_element_type=F32)
    second = jnp.dot(change[:MEM], g_low, preferred_element_type=F32)
    return first[:MEM] + first[MEM:] + second


def turn_operands(prior, value, variance):
    centre = jnp.sum(prior, 0, keepdims=True) * (1.0 / MEM)
    anom = prior - centre
    spread = jnp.sum(anom * anom, 0, keepdims=True) / (MEM - 1) + epsilon
    denom = spread + variance
    post = (variance * centre + spread * value) / denom
    factor = jnp.sqrt(variance / denom)
    change = post + factor * anom - prior
    scaled = anom * (1.0 / ((MEM - 1) * spread))
    high = scaled.astype(BF16).astype(F32)
    low = scaled - high
    left = jnp.concatenate([high, low, high], 0).T.astype(BF16)
    c_high, c_low = split2(change)
    return left, jnp.concatenate([c_high, c_low], 0)


def pick_kernel(order, owner, cells, ens, out, held, pieces, total, sems):
    here = lax.axis_index("region")
    depth = COLS_REG // 4
    out[...] = jnp.zeros_like(out)
    some = functools.reduce(jnp.logical_or, [owner[order[t]] == here for t in range(TURNS)])

    def columns_of(k):
        return pl.ds(pl.multiple_of(k * depth, depth), depth)

    def fetch(k):
        return pltpu.make_async_copy(ens.at[:, columns_of(k)], held.at[k], sems.at[k])

    def cell_of(t):
        return cells[pl.ds(order[t], 1), :]

    @pl.when(some)
    def _():
        for k in range(4):
            fetch(k).start()

        def part(k, _):
            fetch(k).wait()
            value = held[k]
            high = value.astype(BF16)
            middle, low = split2(value - high.astype(F32))
            pieces[...] = jnp.concatenate([high, middle, low], 0)

            def batch(t, _):
                @pl.when(owner[order[t]] == here)
                def _():
                    column = cell_of(t) & (COLS_REG - 1)
                    rows = lax.broadcasted_iota(jnp.int32, (depth, OBS), 0) + k * depth
                    select = jnp.where(rows == column, 1.0, 0.0).astype(BF16)
                    got = jnp.dot(pieces[...], select, preferred_element_type=F32)
                    n = SLAB * STACK
                    got = got[:n] + got[n:2 * n] + got[2 * n:]
                    total[t] = jnp.where(k == 0, got, total[t] + got)

                return 0

            lax.fori_loop(0, TURNS, batch, 0)
            return 0

        lax.fori_loop(0, 4, part, 0)

        def finish(t, _):
            @pl.when(owner[order[t]] == here)
            def _():
                levels = lax.broadcasted_iota(jnp.int32, (SLAB, STACK, OBS), 1)
                values = total[t].reshape(SLAB, STACK, OBS)
                level = (cell_of(t) >> 11)[None]
                out[t, 0:SLAB, :] = jnp.sum(jnp.where(levels == level, values, 0.0), 1)

            return 0

        lax.fori_loop(0, TURNS, finish, 0)


def places():
    region, z = lax.axis_index("region"), lax.axis_index("grp")
    return region // 8, (region // 2) % 4, region % 2, z


def peer(axis, k):
    x, y, c, z = places()
    if axis == "x":
        x = lax.rem(x + k, 4)
    elif axis == "y":
        y = lax.rem(y + k, 4)
    elif axis == "z":
        z = lax.rem(z + k, 4)
    else:
        c = 1 - c
    return (x * 8 + y * 2 + c, z)


def remote(src, dst, send, recv, device):
    return pltpu.make_async_remote_copy(src, dst, send, recv, device_id=device, device_id_type=MESH)


def started(copies):
    for copy in copies:
        copy.start()
    return copies


def wait(copies):
    for copy in copies:
        copy.wait()


def swap_halves(src, dst, sems, k):
    return started([remote(src, dst, sems.at[2 * k], sems.at[2 * k + 1], peer("c", 1))])


def all_sum(a, b, rows, twice, sib, in0, in1, in2, sib_sem, send, recv):
    x, y, c, z = places()
    at = {"x": x, "y": y}
    orders = (("x", "y"), ("y", "x"))
    h = rows // 2
    t = h // 2
    q = t // 4
    r = q // 4 if twice else q
    base, other = pl.multiple_of(c * h, 8), pl.multiple_of((1 - c) * h, 8)
    block = [pl.multiple_of(base + i * t, 8) for i in range(2)]
    quarter = [pl.multiple_of(block[i] + at[orders[i][0]] * q, 8) for i in range(2)]
    own = quarter
    if twice:
        own = [pl.multiple_of(quarter[i] + at[orders[i][1]] * r, 8) for i in range(2)]

    copies = swap_halves(a.at[pl.ds(other, h)], sib, sib_sem, 0)
    yield
    wait(copies)
    a[pl.ds(base, h), :] += sib[...]

    def exchange(phase, pick, inbox, axis_of):
        return started([
            remote(a.at[pl.ds(pick(i, k), inbox.shape[2])], inbox.at[i, k - 1], send.at[phase, i, k - 1],
                   recv.at[phase, i, k - 1], peer(axis_of(i), k))
            for k in (1, 2, 3) for i in range(2)])

    def added(i, at, inbox):
        return a[pl.ds(at, inbox.shape[2]), :] + inbox[i, 0] + inbox[i, 1] + inbox[i, 2]

    copies = exchange(0, lambda i, k: pl.multiple_of(block[i] + lax.rem(at[orders[i][0]] + k, 4) * q, 8),
                      in0, lambda i: orders[i][0])
    yield
    wait(copies)
    for i in range(2):
        a[pl.ds(quarter[i], q), :] = added(i, quarter[i], in0)

    def second(i, k):
        if twice:
            return pl.multiple_of(quarter[i] + lax.rem(at[orders[i][1]] + k, 4) * r, 8)
        return quarter[i]

    copies = exchange(1, second, in1, lambda i: orders[i][1])
    yield
    wait(copies)
    for i in range(2):
        a[pl.ds(own[i], r), :] = added(i, own[i], in1)
    copies = exchange(2, lambda i, k: own[i], in2, lambda i: "z")
    yield
    wait(copies)
    for i in range(2):
        b[pl.ds(own[i], r), :] = added(i, own[i], in2)

    def gather(phase, place, size, axis_of):
        return started([
            remote(b.at[pl.ds(place[i], size)], b.at[pl.ds(place[i], size)], send.at[phase, i, k - 1],
                   recv.at[phase, i, k - 1], peer(axis_of(i), k))
            for k in (1, 2, 3) for i in range(2)])

    if twice:
        copies = gather(3, own, r, lambda i: orders[i][1])
        yield
        wait(copies)
    copies = gather(4, quarter, q, lambda i: orders[i][0])
    yield
    wait(copies)
    half = b.at[pl.ds(base, h)]
    copies = swap_halves(half, half, sib_sem, 1)
    yield
    wait(copies)


def prior_sum(mine, half, all_of, sib, in0, in1, sib_sem, send, recv):
    x, y, c, z = places()
    orders = (("x", "y"), ("y", "x"))
    t = X_ROWS // 2
    base, other = pl.multiple_of(c * X_ROWS, 8), pl.multiple_of((1 - c) * X_ROWS, 8)

    copies = swap_halves(mine.at[pl.ds(other, X_ROWS)], sib, sib_sem, 0)
    yield
    wait(copies)
    half[...] = mine[pl.ds(base, X_ROWS), :] + sib[...]
    for phase, inbox in enumerate((in0, in1)):
        copies = started([
            remote(half.at[i * t:(i + 1) * t], inbox.at[i, k - 1], send.at[phase, i, k - 1], recv.at[phase, i, k - 1],
                   peer(orders[i][phase], k))
            for k in (1, 2, 3) for i in range(2)])
        yield
        wait(copies)
        for i in range(2):
            value = half[i * t:(i + 1) * t, :] + inbox[i, 0] + inbox[i, 1] + inbox[i, 2]
            if phase == 0:
                half[i * t:(i + 1) * t, :] = value
            else:
                all_of[c, z, i * t:(i + 1) * t, :] = value
    spot = all_of.at[c, z]
    copies = started([remote(spot, spot, send.at[2, 0, k - 1], recv.at[2, 0, k - 1], peer("z", k)) for k in (1, 2, 3)])
    yield
    wait(copies)
    spot = all_of.at[c]
    copies = swap_halves(spot, spot, sib_sem, 1)
    yield
    wait(copies)


def main_kernel(order, owner, cells, values, variances, weights, picked, ens, out,
                stage, outbox, state, wt, cross, prior, left, change,
                a, a_sum, b, b_sum, d, d_sum, *rest):
    (sib_a, in0_a, in1_a, in2_a, sib_b, in0_b, in1_b, in2_b, sib_d, in0_d, in1_d, in2_d, x_half, x_all, sib_x, in0_x, in1_x,
     go_send, go_recv, go_own, back_send, back_recv, back_own,
     sibsem_a, send_a, recv_a, sibsem_b, send_b, recv_b, sibsem_d, send_d, recv_d,
     sibsem_x, send_x, recv_x) = rest
    region, z = lax.axis_index("region"), lax.axis_index("grp")

    barrier = pltpu.get_barrier_semaphore()
    around = [peer(axis, k) for axis in ("x", "y", "z") for k in (1, 2, 3)] + [peer("c", 1)]
    for device in around:
        pl.semaphore_signal(barrier, 1, device_id=device, device_id_type=MESH)

    def go(q):
        here = pl.ds(pl.multiple_of(z * COLS_DEV + q * CHUNK, 128), CHUNK)
        copies = [pltpu.make_async_copy(ens.at[:, here], stage.at[z, q], go_own.at[q])]
        for k in (1, 2, 3):
            there = pl.ds(pl.multiple_of(lax.rem(z + k, 4) * COLS_DEV + q * CHUNK, 128), CHUNK)
            copies.append(remote(ens.at[:, there], stage.at[z, q], go_send.at[q, k - 1], go_recv.at[q, k - 1],
                                 peer("z", k)))
        return started(copies)

    def back(q):
        there = pl.ds(pl.multiple_of(z * COLS_DEV + q * CHUNK, 128), CHUNK)
        copies = [pltpu.make_async_copy(outbox.at[z, q], out.at[:, there], back_own.at[q])]
        for k in (1, 2, 3):
            copies.append(remote(outbox.at[lax.rem(z + k, 4), q], out.at[:, there],
                                 back_send.at[q, k - 1], back_recv.at[q, k - 1], peer("z", k)))
        return copies

    def turned(t):
        wt[t] = weights[order[t]].astype(F32).T.astype(BF16)

    def select(n):
        column = cells[pl.ds(order[n], 1), :] & (COLS_REG - 1)
        local = jnp.where(owner[order[n]] == region, column - z * COLS_DEV, -1)
        return jnp.where(lax.broadcasted_iota(jnp.int32, (COLS_DEV, OBS), 0) == local, 1.0, 0.0).astype(BF16)

    def at_columns(t, chosen):
        return jnp.dot(wt[t], chosen, preferred_element_type=F32)

    def put_pair(buffer, rows, row, value):
        buffer[row:row + OBS, :] = value[:, :LANES]
        buffer[rows // 2 + row:rows // 2 + row + OBS, :] = value[:, LANES:]

    def get_pair(buffer, rows, row):
        return jnp.concatenate([buffer[row:row + OBS, :], buffer[rows // 2 + row:rows // 2 + row + OBS, :]], 1)

    for t in range(GROUP - 1):
        turned(t)
    for n in range(1, GROUP):
        chosen = select(n)
        for t in range(n):
            put_pair(a, A_ROWS, FIRST_ROW[t, n], at_columns(t, chosen))

    sum_x = prior_sum(picked, x_half, x_all, sib_x, in0_x, in1_x, sibsem_x, send_x, recv_x)
    sum_a = all_sum(a, a_sum, A_ROWS, True, sib_a, in0_a, in1_a, in2_a, sibsem_a, send_a, recv_a)
    sum_b = all_sum(b, b_sum, B_ROWS, True, sib_b, in0_b, in1_b, in2_b, sibsem_b, send_b, recv_b)
    sum_d = all_sum(d, d_sum, D_ROWS, False, sib_d, in0_d, in1_d, in2_d, sibsem_d, send_d, recv_d)

    pl.semaphore_wait(barrier, len(around))
    next(sum_a)
    next(sum_x)
    sent = [go(0), go(1)]
    next(sum_a)
    next(sum_x)
    for t in range(GROUP - 1, TURNS):
        turned(t)
    for n in range(GROUP + 1, TURNS):
        chosen = select(n)
        for t in range(GROUP, n):
            put_pair(b, B_ROWS, SECOND_ROW[t, n], at_columns(t, chosen))
    next(sum_b)
    next(sum_a)
    next(sum_x)
    next(sum_b)
    next(sum_a)
    next(sum_x)
    for n in range(GROUP, TURNS):
        chosen = select(n)
        for t in range(GROUP):
            cross[CROSS_AT[t, n]] = at_columns(t, chosen).astype(BF16)
    d[...] = jnp.zeros_like(d)
    next(sum_a)
    next(sum_x)
    sent += [go(2)]
    next(sum_b)
    next(sum_a)
    next(sum_b)
    next(sum_x, None)
    next(sum_a)
    sent += [go(3)]
    next(sum_a, None)

    def assimilate(t):
        left[t], change[t] = turn_operands(
            prior[t], values[pl.ds(order[t], 1), :], variances[pl.ds(order[t], 1), :])

    def first_prior(n):
        at = (n % 4) * 24
        for k in range(4):
            prior[n, k * SLAB:(k + 1) * SLAB, :] = x_all[n // 4, k, at:at + SLAB, :]

    for n in range(TURNS):
        first_prior(n)
    for t in range(GROUP):
        assimilate(t)
        for n in range(t + 1, TURNS):
            if n < GROUP:
                prior[n] += increment(prior[n], left[t], change[t], get_pair(a_sum, A_ROWS, FIRST_ROW[t, n]))
            else:
                at = (n - GROUP) * 2 * MEM
                step = increment(prior[n], left[t], change[t], cross[CROSS_AT[t, n]].astype(F32))
                d[at:at + MEM, :] += step[:, :LANES]
                d[at + MEM:at + 2 * MEM, :] += step[:, LANES:]
                prior[n] += step
    next(sum_d)
    next(sum_b)

    def turns(q, first, last):
        lanes = pl.ds(pl.multiple_of(q * CHUNK, 128), CHUNK)

        def turn(t, _):
            w_t = jnp.concatenate([wt[t, :, lanes].astype(F32)] * STACK, 1)
            x = state[q]
            state[q] = x + increment(x, left[t], change[t], w_t)
            return 0

        lax.fori_loop(first, last, turn, 0)

    def early(q):
        def level(s, _):
            lanes = pl.ds(pl.multiple_of(s * CHUNK, 128), CHUNK)
            for k in range(4):
                state[q, k * SLAB:(k + 1) * SLAB, lanes] = stage[k, q, pl.ds(s, SLAB, stride=STACK), :]
            return 0

        lax.fori_loop(0, STACK, level, 0)
        turns(q, 0, EARLY[q])

    next(sum_d)
    wait(sent[0])
    early(0)
    next(sum_d)
    next(sum_b)
    wait(sent[1])
    early(1)
    next(sum_d)
    next(sum_b)
    wait(sent[2])
    early(2)
    next(sum_d)
    next(sum_b, None)
    wait(sent[3])
    early(3)
    next(sum_d)
    next(sum_d, None)

    for n in range(GROUP, TURNS):
        first_prior(n)
        at = (n - GROUP) * 2 * MEM
        prior[n] += jnp.concatenate([d_sum[at:at + MEM, :], d_sum[at + MEM:at + 2 * MEM, :]], 1)
    for t in range(GROUP, TURNS):
        assimilate(t)
        for n in range(t + 1, TURNS):
            prior[n] += increment(prior[n], left[t], change[t], get_pair(b_sum, B_ROWS, SECOND_ROW[t, n]))

    def late(q, _):
        turns(q, jnp.where(q == 0, EARLY[0], EARLY[1]), TURNS)

        def level(s, _):
            lanes = pl.ds(pl.multiple_of(s * CHUNK, 128), CHUNK)
            for k in range(4):
                outbox[k, q, pl.ds(s, SLAB, stride=STACK), :] = state[q, k * SLAB:(k + 1) * SLAB, lanes]
            return 0

        lax.fori_loop(0, STACK, level, 0)
        started(back(q))
        return 0

    lax.fori_loop(0, CHUNKS, late, 0)
    for q in range(CHUNKS):
        wait(back(q))


def body(ensemble, loc_weight, obs_value, obs_var, owner_region, obs_cell, batch_order):
    flat = ensemble.reshape(SLAB * STACK, COLS_REG)
    smem, vmem, anywhere = (pl.BlockSpec(memory_space=m) for m in (pltpu.SMEM, pltpu.VMEM, pl.ANY))
    picked = pl.pallas_call(
        pick_kernel,
        out_shape=jax.ShapeDtypeStruct((TURNS, 24, OBS), F32),
        in_specs=[smem, smem, vmem, anywhere],
        out_specs=vmem,
        scratch_shapes=[
            pltpu.VMEM((4, SLAB * STACK, COLS_REG // 4), F32),
            pltpu.VMEM((3 * SLAB * STACK, COLS_REG // 4), BF16),
            pltpu.VMEM((TURNS, SLAB * STACK, OBS), F32),
            pltpu.SemaphoreType.DMA((4,)),
        ],
        compiler_params=pltpu.CompilerParams(vmem_limit_bytes=60 << 20),
        name="pick",
    )(batch_order, owner_region, obs_cell, flat)

    dma = pltpu.SemaphoreType.DMA

    def room(rows, twice):
        return [pltpu.VMEM((rows // 2, LANES), F32)] + [
            pltpu.VMEM((2, 3, rows // cut, LANES), F32) for cut in ((16, 64, 64) if twice else (16, 16, 16))]

    out = pl.pallas_call(
        main_kernel,
        out_shape=jax.ShapeDtypeStruct((SLAB * STACK, COLS_REG), F32),
        in_specs=[smem, smem, vmem, vmem, vmem, vmem, vmem, anywhere],
        out_specs=anywhere,
        scratch_shapes=[
            pltpu.VMEM((4, CHUNKS, SLAB * STACK, CHUNK), F32),
            pltpu.VMEM((4, CHUNKS, SLAB * STACK, CHUNK), F32),
            pltpu.VMEM((CHUNKS, MEM, CELLS), F32),
            pltpu.VMEM((TURNS, OBS, COLS_DEV), BF16),
            pltpu.VMEM((len(CROSS), OBS, OBS), BF16),
            pltpu.VMEM((TURNS, MEM, OBS), F32),
            pltpu.VMEM((TURNS, OBS, 3 * MEM), BF16),
            pltpu.VMEM((TURNS, 2 * MEM, OBS), BF16),
            *[pltpu.VMEM((rows, LANES), F32) for rows in (A_ROWS, A_ROWS, B_ROWS, B_ROWS, D_ROWS, D_ROWS)],
            *room(A_ROWS, True), *room(B_ROWS, True), *room(D_ROWS, False),
            pltpu.VMEM((X_ROWS, OBS), F32), pltpu.VMEM((2, 4, X_ROWS, OBS), F32), pltpu.VMEM((X_ROWS, OBS), F32),
            pltpu.VMEM((2, 3, X_ROWS // 2, OBS), F32), pltpu.VMEM((2, 3, X_ROWS // 2, OBS), F32),
            dma((CHUNKS, 3)), dma((CHUNKS, 3)), dma((CHUNKS,)),
            dma((CHUNKS, 3)), dma((CHUNKS, 3)), dma((CHUNKS,)),
            dma((4,)), dma((5, 2, 3)), dma((5, 2, 3)),
            dma((4,)), dma((5, 2, 3)), dma((5, 2, 3)),
            dma((4,)), dma((5, 2, 3)), dma((5, 2, 3)),
            dma((4,)), dma((3, 2, 3)), dma((3, 2, 3)),
        ],
        compiler_params=pltpu.CompilerParams(
            collective_id=0, has_side_effects=True, vmem_limit_bytes=60 << 20),
        name="filter",
    )(batch_order, owner_region, obs_cell, obs_value, obs_var, loc_weight,
      picked.reshape(TURNS * 24, OBS), flat)
    return out.reshape(SLAB, STACK, COLS_REG)


def solution(mesh):
    return jax.shard_map(
        body,
        mesh=mesh,
        in_specs=(P("grp", None, "region"), P(None, ("region", "grp"), None), P(), P(), P(), P(), P()),
        out_specs=P("grp", None, "region"),
        check_vma=False,
    )
```

```python
import functools

import jax
import jax.numpy as jnp
from jax import lax
from jax.experimental import pallas as pl
from jax.experimental.pallas import tpu as pltpu
from jax.sharding import PartitionSpec as P

epsilon = 1e-05
MESH = pl.DeviceIdType.MESH
F32, BF16 = jnp.float32, jnp.bfloat16

TURNS, OBS, MEM, SLAB, STACK = 8, 256, 80, 20, 16
COLS_REG, COLS_DEV = 2048, 512
GROUP = 4
LANES = 128
FIRST = [(a, b) for b in range(GROUP) for a in range(b)]
SECOND = [(a, b) for b in range(GROUP, TURNS) for a in range(GROUP, b)]
CROSS = [(a, b) for b in range(GROUP, TURNS) for a in range(GROUP)]
FIRST_ROW = {p: i * OBS for i, p in enumerate(FIRST)}
SECOND_ROW = {p: i * OBS for i, p in enumerate(SECOND)}
CROSS_AT = {p: i for i, p in enumerate(CROSS)}
A_ROWS = 2 * len(FIRST) * OBS
B_ROWS = 2 * len(SECOND) * OBS
D_USED = 2 * (TURNS - GROUP) * MEM
D_ROWS = -(-D_USED // 128) * 128
X_ROWS = TURNS * 24 // 2
PIECES = 2
CHUNKS, CHUNK = 4, 128
CELLS = STACK * CHUNK
EARLY = [GROUP, GROUP - 1, GROUP - 1, GROUP - 1]


def split2(value):
    high = value.astype(BF16)
    low = (value - high.astype(F32)).astype(BF16)
    return high, low


def increment(x, left, change, weights):
    anom = x - jnp.sum(x, 0, keepdims=True) * (1.0 / MEM)
    high, low = split2(anom)
    stacked = jnp.concatenate([high, high, low], 0)
    gain = jnp.dot(left, stacked, preferred_element_type=F32) * weights
    g_high, g_low = split2(gain)
    first = jnp.dot(change, g_high, preferred_element_type=F32)
    second = jnp.dot(change[:MEM], g_low, preferred_element_type=F32)
    return first[:MEM] + first[MEM:] + second


def turn_operands(prior, value, variance):
    centre = jnp.sum(prior, 0, keepdims=True) * (1.0 / MEM)
    anom = prior - centre
    spread = jnp.sum(anom * anom, 0, keepdims=True) / (MEM - 1) + epsilon
    denom = spread + variance
    post = (variance * centre + spread * value) / denom
    factor = jnp.sqrt(variance / denom)
    change = post + factor * anom - prior
    scaled = anom * (1.0 / ((MEM - 1) * spread))
    high = scaled.astype(BF16).astype(F32)
    low = scaled - high
    left = jnp.concatenate([high, low, high], 0).T.astype(BF16)
    c_high, c_low = split2(change)
    return left, jnp.concatenate([c_high, c_low], 0)


def places():
    region, z = lax.axis_index("region"), lax.axis_index("grp")
    return region // 8, (region // 2) % 4, region % 2, z


def peer(axis, k):
    x, y, c, z = places()
    if axis == "x":
        x = lax.rem(x + k, 4)
    elif axis == "y":
        y = lax.rem(y + k, 4)
    elif axis == "z":
        z = lax.rem(z + k, 4)
    else:
        c = 1 - c
    return (x * 8 + y * 2 + c, z)


def remote(src, dst, send, recv, device):
    return pltpu.make_async_remote_copy(src, dst, send, recv, device_id=device, device_id_type=MESH)


def started(copies):
    for copy in copies:
        copy.start()
    return copies


def wait(copies):
    for copy in copies:
        copy.wait()


def swap_halves(src, dst, sems, k):
    return started([remote(src, dst, sems.at[2 * k], sems.at[2 * k + 1], peer("c", 1))])


def all_sum(a, b, rows, twice, sib, in0, in1, in2, sib_sem, send, recv):
    x, y, c, z = places()
    at = {"x": x, "y": y}
    orders = (("x", "y"), ("y", "x"))
    h = rows // 2
    t = h // 2
    q = t // 4
    r = q // 4 if twice else q
    base, other = pl.multiple_of(c * h, 8), pl.multiple_of((1 - c) * h, 8)
    block = [pl.multiple_of(base + i * t, 8) for i in range(2)]
    quarter = [pl.multiple_of(block[i] + at[orders[i][0]] * q, 8) for i in range(2)]
    own = quarter
    if twice:
        own = [pl.multiple_of(quarter[i] + at[orders[i][1]] * r, 8) for i in range(2)]

    copies = swap_halves(a.at[pl.ds(other, h)], sib, sib_sem, 0)
    yield
    wait(copies)
    a[pl.ds(base, h), :] += sib[...]

    def exchange(phase, pick, inbox, axis_of):
        return started([
            remote(a.at[pl.ds(pick(i, k), inbox.shape[2])], inbox.at[i, k - 1], send.at[phase, i, k - 1],
                   recv.at[phase, i, k - 1], peer(axis_of(i), k))
            for k in (1, 2, 3) for i in range(2)])

    def added(i, at, inbox):
        return a[pl.ds(at, inbox.shape[2]), :] + inbox[i, 0] + inbox[i, 1] + inbox[i, 2]

    copies = exchange(0, lambda i, k: pl.multiple_of(block[i] + lax.rem(at[orders[i][0]] + k, 4) * q, 8),
                      in0, lambda i: orders[i][0])
    yield
    wait(copies)
    for i in range(2):
        a[pl.ds(quarter[i], q), :] = added(i, quarter[i], in0)

    def second(i, k):
        if twice:
            return pl.multiple_of(quarter[i] + lax.rem(at[orders[i][1]] + k, 4) * r, 8)
        return quarter[i]

    copies = exchange(1, second, in1, lambda i: orders[i][1])
    yield
    wait(copies)
    for i in range(2):
        a[pl.ds(own[i], r), :] = added(i, own[i], in1)
    copies = exchange(2, lambda i, k: own[i], in2, lambda i: "z")
    yield
    wait(copies)
    for i in range(2):
        b[pl.ds(own[i], r), :] = added(i, own[i], in2)

    def gather(phase, place, size, axis_of):
        return started([
            remote(b.at[pl.ds(place[i], size)], b.at[pl.ds(place[i], size)], send.at[phase, i, k - 1],
                   recv.at[phase, i, k - 1], peer(axis_of(i), k))
            for k in (1, 2, 3) for i in range(2)])

    if twice:
        copies = gather(3, own, r, lambda i: orders[i][1])
        yield
        wait(copies)
    copies = gather(4, quarter, q, lambda i: orders[i][0])
    yield
    wait(copies)
    half = b.at[pl.ds(base, h)]
    copies = swap_halves(half, half, sib_sem, 1)
    yield
    wait(copies)


def prior_sum(mine, half, all_of, sib, in0, in1, sib_sem, send, recv):
    x, y, c, z = places()
    orders = (("x", "y"), ("y", "x"))
    t = X_ROWS // 2
    base, other = pl.multiple_of(c * X_ROWS, 8), pl.multiple_of((1 - c) * X_ROWS, 8)

    copies = swap_halves(mine.at[pl.ds(other, X_ROWS)], sib, sib_sem, 0)
    yield
    wait(copies)
    half[...] = mine[pl.ds(base, X_ROWS), :] + sib[...]
    for phase, inbox in enumerate((in0, in1)):
        copies = started([
            remote(half.at[i * t:(i + 1) * t], inbox.at[i, k - 1], send.at[phase, i, k - 1], recv.at[phase, i, k - 1],
                   peer(orders[i][phase], k))
            for k in (1, 2, 3) for i in range(2)])
        yield
        wait(copies)
        for i in range(2):
            value = half[i * t:(i + 1) * t, :] + inbox[i, 0] + inbox[i, 1] + inbox[i, 2]
            if phase == 0:
                half[i * t:(i + 1) * t, :] = value
            else:
                all_of[c, z, i * t:(i + 1) * t, :] = value
    spot = all_of.at[c, z]
    copies = started([remote(spot, spot, send.at[2, 0, k - 1], recv.at[2, 0, k - 1], peer("z", k)) for k in (1, 2, 3)])
    yield
    wait(copies)
    spot = all_of.at[c]
    copies = swap_halves(spot, spot, sib_sem, 1)
    yield
    wait(copies)


def main_kernel(order_in, owner_in, cells_in, values_in, variances_in, weights_in, ens, out,
                order, owner, cells, values, variances, weights, held, pieces, picked,
                stage, outbox, state, wt, cross, prior, left, change,
                a, a_sum, b, b_sum, d, d_sum, *rest):
    (sib_a, in0_a, in1_a, in2_a, sib_b, in0_b, in1_b, in2_b, sib_d, in0_d, in1_d, in2_d, x_half, x_all, sib_x, in0_x, in1_x,
     go_send, go_recv, go_own, back_send, back_recv, back_own,
     sibsem_a, send_a, recv_a, sibsem_b, send_b, recv_b, sibsem_d, send_d, recv_d,
     sibsem_x, send_x, recv_x, in_sems, held_sems) = rest
    region, z = lax.axis_index("region"), lax.axis_index("grp")

    barrier = pltpu.get_barrier_semaphore()
    around = [peer(axis, k) for axis in ("x", "y", "z") for k in (1, 2, 3)] + [peer("c", 1)]
    for device in around:
        pl.semaphore_signal(barrier, 1, device_id=device, device_id_type=MESH)

    arrays = ((order_in, order), (owner_in, owner), (cells_in, cells), (weights_in, weights),
              (values_in, values), (variances_in, variances))
    loads = started([pltpu.make_async_copy(src, dst, in_sems.at[i]) for i, (src, dst) in enumerate(arrays)])
    blocks = started([
        pltpu.make_async_copy(ens.at[:, k * COLS_DEV:(k + 1) * COLS_DEV], held.at[k], held_sems.at[k]) for k in range(4)])
    wait(loads)

    def go(q):
        here = pl.ds(pl.multiple_of(z * COLS_DEV + q * CHUNK, 128), CHUNK)
        copies = [pltpu.make_async_copy(ens.at[:, here], stage.at[z, q], go_own.at[q])]
        for k in (1, 2, 3):
            there = pl.ds(pl.multiple_of(lax.rem(z + k, 4) * COLS_DEV + q * CHUNK, 128), CHUNK)
            copies.append(remote(ens.at[:, there], stage.at[z, q], go_send.at[q, k - 1], go_recv.at[q, k - 1],
                                 peer("z", k)))
        return started(copies)

    def back(q):
        there = pl.ds(pl.multiple_of(z * COLS_DEV + q * CHUNK, 128), CHUNK)
        copies = [pltpu.make_async_copy(outbox.at[z, q], out.at[:, there], back_own.at[q])]
        for k in (1, 2, 3):
            copies.append(remote(outbox.at[lax.rem(z + k, 4), q], out.at[:, there],
                                 back_send.at[q, k - 1], back_recv.at[q, k - 1], peer("z", k)))
        return copies

    def turned(t):
        wt[t] = weights[order[t]].astype(F32).T.astype(BF16)

    def select(n):
        column = cells[pl.ds(order[n], 1), :] & (COLS_REG - 1)
        local = jnp.where(owner[order[n]] == region, column - z * COLS_DEV, -1)
        return jnp.where(lax.broadcasted_iota(jnp.int32, (COLS_DEV, OBS), 0) == local, 1.0, 0.0).astype(BF16)

    def at_columns(t, chosen):
        return jnp.dot(wt[t], chosen, preferred_element_type=F32)

    def put_pair(buffer, rows, row, value):
        buffer[row:row + OBS, :] = value[:, :LANES]
        buffer[rows // 2 + row:rows // 2 + row + OBS, :] = value[:, LANES:]

    def get_pair(buffer, rows, row):
        return jnp.concatenate([buffer[row:row + OBS, :], buffer[rows // 2 + row:rows // 2 + row + OBS, :]], 1)

    for t in range(GROUP - 1):
        turned(t)
    for n in range(1, GROUP):
        chosen = select(n)
        for t in range(n):
            put_pair(a, A_ROWS, FIRST_ROW[t, n], at_columns(t, chosen))

    sum_x = prior_sum(picked, x_half, x_all, sib_x, in0_x, in1_x, sibsem_x, send_x, recv_x)
    sum_a = all_sum(a, a_sum, A_ROWS, True, sib_a, in0_a, in1_a, in2_a, sibsem_a, send_a, recv_a)
    sum_b = all_sum(b, b_sum, B_ROWS, True, sib_b, in0_b, in1_b, in2_b, sibsem_b, send_b, recv_b)
    sum_d = all_sum(d, d_sum, D_ROWS, False, sib_d, in0_d, in1_d, in2_d, sibsem_d, send_d, recv_d)

    def pick(n, _):
        cell = cells[pl.ds(order[n], 1), :]
        column = jnp.where(owner[order[n]] == region, cell & (COLS_REG - 1), -1)
        total = jnp.zeros((SLAB * STACK, OBS), F32)
        for k in range(4):
            rows = lax.broadcasted_iota(jnp.int32, (COLS_DEV, OBS), 0) + k * COLS_DEV
            chosen = jnp.where(rows == column, 1.0, 0.0).astype(BF16)
            got = jnp.dot(pieces[k], chosen, preferred_element_type=F32)
            for i in range(PIECES):
                total = total + got[i * SLAB * STACK:(i + 1) * SLAB * STACK]
        levels = lax.broadcasted_iota(jnp.int32, (SLAB, STACK, OBS), 1)
        value = jnp.where(levels == (cell >> 11)[None], total.reshape(SLAB, STACK, OBS), 0.0)
        picked[pl.ds(pl.multiple_of(n * 24, 8), SLAB), :] = jnp.sum(value, 1)
        return 0

    pl.semaphore_wait(barrier, len(around))
    next(sum_a)
    sent = [go(0), go(1)]
    picked[...] = jnp.zeros_like(picked)
    for k in range(4):
        wait(blocks[k:k + 1])
        rest_of = held[k]
        for i in range(PIECES):
            piece = rest_of.astype(BF16)
            pieces[k, i * SLAB * STACK:(i + 1) * SLAB * STACK, :] = piece
            rest_of = rest_of - piece.astype(F32)
    next(sum_a)
    lax.fori_loop(0, 6, pick, 0)
    next(sum_a)
    lax.fori_loop(6, TURNS, pick, 0)
    next(sum_x)
    for t in range(GROUP - 1, TURNS):
        turned(t)
    next(sum_x)
    next(sum_a)
    for n in range(GROUP + 1, TURNS):
        chosen = select(n)
        for t in range(GROUP, n):
            put_pair(b, B_ROWS, SECOND_ROW[t, n], at_columns(t, chosen))
    next(sum_b)
    next(sum_x)
    next(sum_a)
    next(sum_b)
    for n in range(GROUP, TURNS):
        chosen = select(n)
        for t in range(GROUP):
            cross[CROSS_AT[t, n]] = at_columns(t, chosen).astype(BF16)
    d[...] = jnp.zeros_like(d)
    next(sum_x)
    next(sum_a)
    next(sum_b)
    next(sum_x)
    sent += [go(2)]
    next(sum_a)
    next(sum_b)
    next(sum_x, None)
    next(sum_a, None)

    def assimilate(t):
        left[t], change[t] = turn_operands(
            prior[t], values[pl.ds(order[t], 1), :], variances[pl.ds(order[t], 1), :])

    def first_prior(n):
        at = (n % 4) * 24
        for k in range(4):
            prior[n, k * SLAB:(k + 1) * SLAB, :] = x_all[n // 4, k, at:at + SLAB, :]

    for n in range(TURNS):
        first_prior(n)
    for t in range(GROUP):
        assimilate(t)
        for n in range(t + 1, TURNS):
            if n < GROUP:
                prior[n] += increment(prior[n], left[t], change[t], get_pair(a_sum, A_ROWS, FIRST_ROW[t, n]))
            else:
                at = (n - GROUP) * 2 * MEM
                step = increment(prior[n], left[t], change[t], cross[CROSS_AT[t, n]].astype(F32))
                d[at:at + MEM, :] += step[:, :LANES]
                d[at + MEM:at + 2 * MEM, :] += step[:, LANES:]
                prior[n] += step
    next(sum_d)

    def turns(q, first, last):
        lanes = pl.ds(pl.multiple_of(q * CHUNK, 128), CHUNK)

        def turn(t, _):
            w_t = jnp.concatenate([wt[t, :, lanes].astype(F32)] * STACK, 1)
            x = state[q]
            state[q] = x + increment(x, left[t], change[t], w_t)
            return 0

        lax.fori_loop(first, last, turn, 0)

    def early(q):
        def level(s, _):
            lanes = pl.ds(pl.multiple_of(s * CHUNK, 128), CHUNK)
            for k in range(4):
                state[q, k * SLAB:(k + 1) * SLAB, lanes] = stage[k, q, pl.ds(s, SLAB, stride=STACK), :]
            return 0

        lax.fori_loop(0, STACK, level, 0)
        turns(q, 0, EARLY[q])

    next(sum_d)
    next(sum_b)
    sent += [go(3)]
    wait(sent[0])
    early(0)
    next(sum_d)
    wait(sent[1])
    early(1)
    next(sum_b)
    next(sum_d)
    wait(sent[2])
    early(2)
    next(sum_d)
    next(sum_b)
    wait(sent[3])
    early(3)
    next(sum_d)
    next(sum_b, None)
    next(sum_d, None)

    for n in range(GROUP, TURNS):
        first_prior(n)
        at = (n - GROUP) * 2 * MEM
        prior[n] += jnp.concatenate([d_sum[at:at + MEM, :], d_sum[at + MEM:at + 2 * MEM, :]], 1)
    for t in range(GROUP, TURNS):
        assimilate(t)
        for n in range(t + 1, TURNS):
            prior[n] += increment(prior[n], left[t], change[t], get_pair(b_sum, B_ROWS, SECOND_ROW[t, n]))

    def late(q, _):
        turns(q, jnp.where(q == 0, EARLY[0], EARLY[1]), TURNS)

        def level(s, _):
            lanes = pl.ds(pl.multiple_of(s * CHUNK, 128), CHUNK)
            for k in range(4):
                outbox[k, q, pl.ds(s, SLAB, stride=STACK), :] = state[q, k * SLAB:(k + 1) * SLAB, lanes]
            return 0

        lax.fori_loop(0, STACK, level, 0)
        started(back(q))
        return 0

    lax.fori_loop(0, CHUNKS, late, 0)
    for q in range(CHUNKS):
        wait(back(q))


def body(ensemble, loc_weight, obs_value, obs_var, owner_region, obs_cell, batch_order):
    flat = ensemble.reshape(SLAB * STACK, COLS_REG)
    dma = pltpu.SemaphoreType.DMA

    def room(rows, twice):
        return [pltpu.VMEM((rows // 2, LANES), F32)] + [
            pltpu.VMEM((2, 3, rows // cut, LANES), F32) for cut in ((16, 64, 64) if twice else (16, 16, 16))]

    out = pl.pallas_call(
        main_kernel,
        out_shape=jax.ShapeDtypeStruct((SLAB * STACK, COLS_REG), F32),
        in_specs=[pl.BlockSpec(memory_space=pltpu.HBM)] * 7,
        out_specs=pl.BlockSpec(memory_space=pl.ANY),
        scratch_shapes=[
            pltpu.SMEM((TURNS,), jnp.int32), pltpu.SMEM((TURNS,), jnp.int32), pltpu.VMEM((TURNS, OBS), jnp.int32),
            pltpu.VMEM((TURNS, OBS), F32), pltpu.VMEM((TURNS, OBS), F32),
            pltpu.VMEM((TURNS, COLS_DEV, OBS), BF16),
            pltpu.VMEM((4, SLAB * STACK, COLS_DEV), F32),
            pltpu.VMEM((4, PIECES * SLAB * STACK, COLS_DEV), BF16),
            pltpu.VMEM((TURNS * 24, OBS), F32),
            pltpu.VMEM((4, CHUNKS, SLAB * STACK, CHUNK), F32),
            pltpu.VMEM((4, CHUNKS, SLAB * STACK, CHUNK), F32),
            pltpu.VMEM((CHUNKS, MEM, CELLS), F32),
            pltpu.VMEM((TURNS, OBS, COLS_DEV), BF16),
            pltpu.VMEM((len(CROSS), OBS, OBS), BF16),
            pltpu.VMEM((TURNS, MEM, OBS), F32),
            pltpu.VMEM((TURNS, OBS, 3 * MEM), BF16),
            pltpu.VMEM((TURNS, 2 * MEM, OBS), BF16),
            *[pltpu.VMEM((rows, LANES), F32) for rows in (A_ROWS, A_ROWS, B_ROWS, B_ROWS, D_ROWS, D_ROWS)],
            *room(A_ROWS, True), *room(B_ROWS, True), *room(D_ROWS, False),
            pltpu.VMEM((X_ROWS, OBS), F32), pltpu.VMEM((2, 4, X_ROWS, OBS), F32), pltpu.VMEM((X_ROWS, OBS), F32),
            pltpu.VMEM((2, 3, X_ROWS // 2, OBS), F32), pltpu.VMEM((2, 3, X_ROWS // 2, OBS), F32),
            dma((CHUNKS, 3)), dma((CHUNKS, 3)), dma((CHUNKS,)),
            dma((CHUNKS, 3)), dma((CHUNKS, 3)), dma((CHUNKS,)),
            dma((4,)), dma((5, 2, 3)), dma((5, 2, 3)),
            dma((4,)), dma((5, 2, 3)), dma((5, 2, 3)),
            dma((4,)), dma((5, 2, 3)), dma((5, 2, 3)),
            dma((4,)), dma((3, 2, 3)), dma((3, 2, 3)),
            dma((6,)), dma((4,)),
        ],
        compiler_params=pltpu.CompilerParams(
            collective_id=0, has_side_effects=True, vmem_limit_bytes=60 << 20),
        name="filter",
    )(batch_order, owner_region, obs_cell, obs_value, obs_var, loc_weight, flat)
    return out.reshape(SLAB, STACK, COLS_REG)


def solution(mesh):
    return jax.shard_map(
        body,
        mesh=mesh,
        in_specs=(P("grp", None, "region"), P(None, ("region", "grp"), None), P(), P(), P(), P(), P()),
        out_specs=P("grp", None, "region"),
        check_vma=False,
    )
```

```python
import functools

import jax
import jax.numpy as jnp
from jax import lax
from jax.experimental import pallas as pl
from jax.experimental.pallas import tpu as pltpu
from jax.sharding import PartitionSpec as P

epsilon = 1e-05
MESH = pl.DeviceIdType.MESH
F32, BF16 = jnp.float32, jnp.bfloat16

TURNS, OBS, MEM, SLAB, STACK = 8, 256, 80, 20, 16
COLS_REG, COLS_DEV = 2048, 512
GROUP = 4
LANES = 128
FIRST = [(a, b) for b in range(GROUP) for a in range(b)]
SECOND = [(a, b) for b in range(GROUP, TURNS) for a in range(GROUP, b)]
CROSS = [(a, b) for b in range(GROUP, TURNS) for a in range(GROUP)]
FIRST_ROW = {p: i * OBS for i, p in enumerate(FIRST)}
SECOND_ROW = {p: i * OBS for i, p in enumerate(SECOND)}
CROSS_AT = {p: i for i, p in enumerate(CROSS)}
A_ROWS = 2 * len(FIRST) * OBS
B_ROWS = 2 * len(SECOND) * OBS
D_USED = 2 * (TURNS - GROUP) * MEM
D_ROWS = -(-D_USED // 128) * 128
X_ROWS = TURNS * 24 // 2
PIECES = 2
CHUNKS, CHUNK = 4, 128
CELLS = STACK * CHUNK
EARLY = [GROUP, GROUP - 1, GROUP - 1, GROUP - 1]


def split2(value):
    high = value.astype(BF16)
    low = (value - high.astype(F32)).astype(BF16)
    return high, low


def increment(x, left, change, weights):
    anom = x - jnp.sum(x, 0, keepdims=True) * (1.0 / MEM)
    high, low = split2(anom)
    stacked = jnp.concatenate([high, high, low], 0)
    gain = jnp.dot(left, stacked, preferred_element_type=F32) * weights
    g_high, g_low = split2(gain)
    first = jnp.dot(change, g_high, preferred_element_type=F32)
    second = jnp.dot(change[:MEM], g_low, preferred_element_type=F32)
    return first[:MEM] + first[MEM:] + second


def turn_operands(prior, value, variance):
    centre = jnp.sum(prior, 0, keepdims=True) * (1.0 / MEM)
    anom = prior - centre
    spread = jnp.sum(anom * anom, 0, keepdims=True) / (MEM - 1) + epsilon
    denom = spread + variance
    post = (variance * centre + spread * value) / denom
    factor = jnp.sqrt(variance / denom)
    change = post + factor * anom - prior
    scaled = anom * (1.0 / ((MEM - 1) * spread))
    high = scaled.astype(BF16).astype(F32)
    low = scaled - high
    left = jnp.concatenate([high, low, high], 0).T.astype(BF16)
    c_high, c_low = split2(change)
    return left, jnp.concatenate([c_high, c_low], 0)


def places():
    region, z = lax.axis_index("region"), lax.axis_index("grp")
    return region // 8, (region // 2) % 4, region % 2, z


def peer(axis, k):
    x, y, c, z = places()
    if axis == "x":
        x = lax.rem(x + k, 4)
    elif axis == "y":
        y = lax.rem(y + k, 4)
    elif axis == "z":
        z = lax.rem(z + k, 4)
    else:
        c = 1 - c
    return (x * 8 + y * 2 + c, z)


def remote(src, dst, send, recv, device):
    return pltpu.make_async_remote_copy(src, dst, send, recv, device_id=device, device_id_type=MESH)


def started(copies):
    for copy in copies:
        copy.start()
    return copies


def wait(copies):
    for copy in copies:
        copy.wait()


def swap_halves(src, dst, sems, k):
    return started([remote(src, dst, sems.at[2 * k], sems.at[2 * k + 1], peer("c", 1))])


def all_sum(a, b, rows, twice, sib, in0, in1, in2, sib_sem, send, recv):
    x, y, c, z = places()
    at = {"x": x, "y": y}
    orders = (("x", "y"), ("y", "x"))
    h = rows // 2
    t = h // 2
    q = t // 4
    r = q // 4 if twice else q
    base, other = pl.multiple_of(c * h, 8), pl.multiple_of((1 - c) * h, 8)
    block = [pl.multiple_of(base + i * t, 8) for i in range(2)]
    quarter = [pl.multiple_of(block[i] + at[orders[i][0]] * q, 8) for i in range(2)]
    own = quarter
    if twice:
        own = [pl.multiple_of(quarter[i] + at[orders[i][1]] * r, 8) for i in range(2)]

    copies = swap_halves(a.at[pl.ds(other, h)], sib, sib_sem, 0)
    yield
    wait(copies)
    a[pl.ds(base, h), :] += sib[...]

    def exchange(phase, pick, inbox, axis_of):
        return started([
            remote(a.at[pl.ds(pick(i, k), inbox.shape[2])], inbox.at[i, k - 1], send.at[phase, i, k - 1],
                   recv.at[phase, i, k - 1], peer(axis_of(i), k))
            for k in (1, 2, 3) for i in range(2)])

    def added(i, at, inbox):
        return a[pl.ds(at, inbox.shape[2]), :] + inbox[i, 0] + inbox[i, 1] + inbox[i, 2]

    copies = exchange(0, lambda i, k: pl.multiple_of(block[i] + lax.rem(at[orders[i][0]] + k, 4) * q, 8),
                      in0, lambda i: orders[i][0])
    yield
    wait(copies)
    for i in range(2):
        a[pl.ds(quarter[i], q), :] = added(i, quarter[i], in0)

    def second(i, k):
        if twice:
            return pl.multiple_of(quarter[i] + lax.rem(at[orders[i][1]] + k, 4) * r, 8)
        return quarter[i]

    copies = exchange(1, second, in1, lambda i: orders[i][1])
    yield
    wait(copies)
    for i in range(2):
        a[pl.ds(own[i], r), :] = added(i, own[i], in1)
    copies = exchange(2, lambda i, k: own[i], in2, lambda i: "z")
    yield
    wait(copies)
    for i in range(2):
        b[pl.ds(own[i], r), :] = added(i, own[i], in2)

    def gather(phase, place, size, axis_of):
        return started([
            remote(b.at[pl.ds(place[i], size)], b.at[pl.ds(place[i], size)], send.at[phase, i, k - 1],
                   recv.at[phase, i, k - 1], peer(axis_of(i), k))
            for k in (1, 2, 3) for i in range(2)])

    if twice:
        copies = gather(3, own, r, lambda i: orders[i][1])
        yield
        wait(copies)
    copies = gather(4, quarter, q, lambda i: orders[i][0])
    yield
    wait(copies)
    half = b.at[pl.ds(base, h)]
    copies = swap_halves(half, half, sib_sem, 1)
    yield
    wait(copies)


def prior_sum(mine, half, all_of, sib, in0, in1, sib_sem, send, recv):
    x, y, c, z = places()
    orders = (("x", "y"), ("y", "x"))
    t = X_ROWS // 2
    base, other = pl.multiple_of(c * X_ROWS, 8), pl.multiple_of((1 - c) * X_ROWS, 8)

    copies = swap_halves(mine.at[pl.ds(other, X_ROWS)], sib, sib_sem, 0)
    yield
    wait(copies)
    half[...] = mine[pl.ds(base, X_ROWS), :] + sib[...]
    for phase, inbox in enumerate((in0, in1)):
        copies = started([
            remote(half.at[i * t:(i + 1) * t], inbox.at[i, k - 1], send.at[phase, i, k - 1], recv.at[phase, i, k - 1],
                   peer(orders[i][phase], k))
            for k in (1, 2, 3) for i in range(2)])
        yield
        wait(copies)
        for i in range(2):
            value = half[i * t:(i + 1) * t, :] + inbox[i, 0] + inbox[i, 1] + inbox[i, 2]
            if phase == 0:
                half[i * t:(i + 1) * t, :] = value
            else:
                all_of[c, z, i * t:(i + 1) * t, :] = value
    spot = all_of.at[c, z]
    copies = started([remote(spot, spot, send.at[2, 0, k - 1], recv.at[2, 0, k - 1], peer("z", k)) for k in (1, 2, 3)])
    yield
    wait(copies)
    spot = all_of.at[c]
    copies = swap_halves(spot, spot, sib_sem, 1)
    yield
    wait(copies)


def main_kernel(order_in, owner_in, cells_in, values_in, variances_in, weights_in, ens, out,
                order, owner, cells, values, variances, weights, held, pieces, picked,
                stage, outbox, state, wt, cross, prior, left, change,
                a, a_sum, b, b_sum, d, d_sum, *rest):
    (sib_a, in0_a, in1_a, in2_a, sib_b, in0_b, in1_b, in2_b, sib_d, in0_d, in1_d, in2_d, x_half, x_all, sib_x, in0_x, in1_x,
     go_send, go_recv, go_own, back_send, back_recv, back_own,
     sibsem_a, send_a, recv_a, sibsem_b, send_b, recv_b, sibsem_d, send_d, recv_d,
     sibsem_x, send_x, recv_x, in_sems, held_sems) = rest
    region, z = lax.axis_index("region"), lax.axis_index("grp")

    barrier = pltpu.get_barrier_semaphore()
    around = [peer(axis, k) for axis in ("x", "y", "z") for k in (1, 2, 3)] + [peer("c", 1)]
    for device in around:
        pl.semaphore_signal(barrier, 1, device_id=device, device_id_type=MESH)

    arrays = ((order_in, order), (owner_in, owner), (cells_in, cells), (weights_in, weights),
              (values_in, values), (variances_in, variances))
    loads = started([pltpu.make_async_copy(src, dst, in_sems.at[i]) for i, (src, dst) in enumerate(arrays)])
    blocks = started([
        pltpu.make_async_copy(ens.at[:, k * COLS_DEV:(k + 1) * COLS_DEV], held.at[k], held_sems.at[k]) for k in range(4)])
    wait(loads)

    def go(q):
        here = pl.ds(pl.multiple_of(z * COLS_DEV + q * CHUNK, 128), CHUNK)
        copies = [pltpu.make_async_copy(ens.at[:, here], stage.at[z, q], go_own.at[q])]
        for k in (1, 2, 3):
            there = pl.ds(pl.multiple_of(lax.rem(z + k, 4) * COLS_DEV + q * CHUNK, 128), CHUNK)
            copies.append(remote(ens.at[:, there], stage.at[z, q], go_send.at[q, k - 1], go_recv.at[q, k - 1],
                                 peer("z", k)))
        return started(copies)

    def back(q):
        there = pl.ds(pl.multiple_of(z * COLS_DEV + q * CHUNK, 128), CHUNK)
        copies = [pltpu.make_async_copy(outbox.at[z, q], out.at[:, there], back_own.at[q])]
        for k in (1, 2, 3):
            copies.append(remote(outbox.at[lax.rem(z + k, 4), q], out.at[:, there],
                                 back_send.at[q, k - 1], back_recv.at[q, k - 1], peer("z", k)))
        return copies

    def turned(t):
        wt[t] = weights[order[t]].astype(F32).T.astype(BF16)

    def select(n):
        column = cells[pl.ds(order[n], 1), :] & (COLS_REG - 1)
        local = jnp.where(owner[order[n]] == region, column - z * COLS_DEV, -1)
        return jnp.where(lax.broadcasted_iota(jnp.int32, (COLS_DEV, OBS), 0) == local, 1.0, 0.0).astype(BF16)

    def at_columns(t, chosen):
        return jnp.dot(wt[t], chosen, preferred_element_type=F32)

    def put_pair(buffer, rows, row, value):
        buffer[row:row + OBS, :] = value[:, :LANES]
        buffer[rows // 2 + row:rows // 2 + row + OBS, :] = value[:, LANES:]

    def get_pair(buffer, rows, row):
        return jnp.concatenate([buffer[row:row + OBS, :], buffer[rows // 2 + row:rows // 2 + row + OBS, :]], 1)

    for t in range(GROUP - 1):
        turned(t)
    for n in range(1, GROUP):
        chosen = select(n)
        for t in range(n):
            put_pair(a, A_ROWS, FIRST_ROW[t, n], at_columns(t, chosen))

    sum_x = prior_sum(picked, x_half, x_all, sib_x, in0_x, in1_x, sibsem_x, send_x, recv_x)
    sum_a = all_sum(a, a_sum, A_ROWS, True, sib_a, in0_a, in1_a, in2_a, sibsem_a, send_a, recv_a)
    sum_b = all_sum(b, b_sum, B_ROWS, True, sib_b, in0_b, in1_b, in2_b, sibsem_b, send_b, recv_b)
    sum_d = all_sum(d, d_sum, D_ROWS, False, sib_d, in0_d, in1_d, in2_d, sibsem_d, send_d, recv_d)

    def pick(n, _):
        cell = cells[pl.ds(order[n], 1), :]
        column = jnp.where(owner[order[n]] == region, cell & (COLS_REG - 1), -1)
        total = jnp.zeros((SLAB * STACK, OBS), F32)
        for k in range(4):
            rows = lax.broadcasted_iota(jnp.int32, (COLS_DEV, OBS), 0) + k * COLS_DEV
            chosen = jnp.where(rows == column, 1.0, 0.0).astype(BF16)
            got = jnp.dot(pieces[k], chosen, preferred_element_type=F32)
            for i in range(PIECES):
                total = total + got[i * SLAB * STACK:(i + 1) * SLAB * STACK]
        levels = lax.broadcasted_iota(jnp.int32, (SLAB, STACK, OBS), 1)
        value = jnp.where(levels == (cell >> 11)[None], total.reshape(SLAB, STACK, OBS), 0.0)
        picked[pl.ds(pl.multiple_of(n * 24, 8), SLAB), :] = jnp.sum(value, 1)
        return 0

    pl.semaphore_wait(barrier, len(around))
    next(sum_a)
    sent = [go(0), go(1)]
    picked[...] = jnp.zeros_like(picked)
    for k in range(4):
        wait(blocks[k:k + 1])
        rest_of = held[k]
        for i in range(PIECES):
            piece = rest_of.astype(BF16)
            pieces[k, i * SLAB * STACK:(i + 1) * SLAB * STACK, :] = piece
            rest_of = rest_of - piece.astype(F32)
    next(sum_a)
    lax.fori_loop(0, 6, pick, 0)
    next(sum_a)
    lax.fori_loop(6, TURNS, pick, 0)
    next(sum_x)
    for t in range(GROUP - 1, TURNS):
        turned(t)
    next(sum_x)
    next(sum_a)
    for n in range(GROUP + 1, TURNS):
        chosen = select(n)
        for t in range(GROUP, n):
            put_pair(b, B_ROWS, SECOND_ROW[t, n], at_columns(t, chosen))
    next(sum_b)
    next(sum_x)
    next(sum_a)
    next(sum_b)
    next(sum_x)
    next(sum_a)
    for n in range(GROUP, TURNS):
        chosen = select(n)
        for t in range(GROUP):
            cross[CROSS_AT[t, n]] = at_columns(t, chosen).astype(BF16)
    d[...] = jnp.zeros_like(d)
    next(sum_x)
    sent += [go(2)]
    next(sum_b)
    next(sum_a)
    next(sum_b)
    next(sum_x, None)
    next(sum_a, None)

    def assimilate(t):
        left[t], change[t] = turn_operands(
            prior[t], values[pl.ds(order[t], 1), :], variances[pl.ds(order[t], 1), :])

    def first_prior(n):
        at = (n % 4) * 24
        for k in range(4):
            prior[n, k * SLAB:(k + 1) * SLAB, :] = x_all[n // 4, k, at:at + SLAB, :]

    for n in range(TURNS):
        first_prior(n)
    for t in range(GROUP):
        assimilate(t)
        for n in range(t + 1, TURNS):
            if n < GROUP:
                prior[n] += increment(prior[n], left[t], change[t], get_pair(a_sum, A_ROWS, FIRST_ROW[t, n]))
            else:
                at = (n - GROUP) * 2 * MEM
                step = increment(prior[n], left[t], change[t], cross[CROSS_AT[t, n]].astype(F32))
                d[at:at + MEM, :] += step[:, :LANES]
                d[at + MEM:at + 2 * MEM, :] += step[:, LANES:]
                prior[n] += step
    next(sum_d)

    def turn(q, t):
        lanes = pl.ds(pl.multiple_of(q * CHUNK, 128), CHUNK)
        w_t = jnp.concatenate([wt[t, :, lanes].astype(F32)] * STACK, 1)
        x = state[q]
        state[q] = x + increment(x, left[t], change[t], w_t)

    def turns(q, first, last):
        def one(t, _):
            turn(q, t)
            return 0

        lax.fori_loop(first, last, one, 0)

    def early(q):
        def level(s, _):
            lanes = pl.ds(pl.multiple_of(s * CHUNK, 128), CHUNK)
            for k in range(4):
                state[q, k * SLAB:(k + 1) * SLAB, lanes] = stage[k, q, pl.ds(s, SLAB, stride=STACK), :]
            return 0

        lax.fori_loop(0, STACK, level, 0)
        turns(q, 0, EARLY[q])

    next(sum_d)
    next(sum_b)
    sent += [go(3)]
    wait(sent[0])
    early(0)
    next(sum_d)
    wait(sent[1])
    early(1)
    next(sum_b)
    next(sum_d)
    wait(sent[2])
    early(2)
    next(sum_d)
    next(sum_b)
    wait(sent[3])
    early(3)
    next(sum_d)
    next(sum_d, None)

    for n in range(GROUP, TURNS):
        first_prior(n)
        at = (n - GROUP) * 2 * MEM
        prior[n] += jnp.concatenate([d_sum[at:at + MEM, :], d_sum[at + MEM:at + 2 * MEM, :]], 1)
    for t in range(GROUP, TURNS):
        assimilate(t)
        if t == GROUP:
            next(sum_b, None)
        for n in range(t + 1, TURNS):
            prior[n] += increment(prior[n], left[t], change[t], get_pair(b_sum, B_ROWS, SECOND_ROW[t, n]))
        turn(0, t)

    def give(q):
        def level(s, _):
            lanes = pl.ds(pl.multiple_of(s * CHUNK, 128), CHUNK)
            for k in range(4):
                outbox[k, q, pl.ds(s, SLAB, stride=STACK), :] = state[q, k * SLAB:(k + 1) * SLAB, lanes]
            return 0

        lax.fori_loop(0, STACK, level, 0)
        started(back(q))

    def late(q, _):
        turns(q, EARLY[1], TURNS)
        give(q)
        return 0

    give(0)
    lax.fori_loop(1, CHUNKS, late, 0)
    for q in range(CHUNKS):
        wait(back(q))


def body(ensemble, loc_weight, obs_value, obs_var, owner_region, obs_cell, batch_order):
    flat = ensemble.reshape(SLAB * STACK, COLS_REG)
    dma = pltpu.SemaphoreType.DMA

    def room(rows, twice):
        return [pltpu.VMEM((rows // 2, LANES), F32)] + [
            pltpu.VMEM((2, 3, rows // cut, LANES), F32) for cut in ((16, 64, 64) if twice else (16, 16, 16))]

    out = pl.pallas_call(
        main_kernel,
        out_shape=jax.ShapeDtypeStruct((SLAB * STACK, COLS_REG), F32),
        in_specs=[pl.BlockSpec(memory_space=pltpu.HBM)] * 7,
        out_specs=pl.BlockSpec(memory_space=pl.ANY),
        scratch_shapes=[
            pltpu.SMEM((TURNS,), jnp.int32), pltpu.SMEM((TURNS,), jnp.int32), pltpu.VMEM((TURNS, OBS), jnp.int32),
            pltpu.VMEM((TURNS, OBS), F32), pltpu.VMEM((TURNS, OBS), F32),
            pltpu.VMEM((TURNS, COLS_DEV, OBS), BF16),
            pltpu.VMEM((4, SLAB * STACK, COLS_DEV), F32),
            pltpu.VMEM((4, PIECES * SLAB * STACK, COLS_DEV), BF16),
            pltpu.VMEM((TURNS * 24, OBS), F32),
            pltpu.VMEM((4, CHUNKS, SLAB * STACK, CHUNK), F32),
            pltpu.VMEM((4, CHUNKS, SLAB * STACK, CHUNK), F32),
            pltpu.VMEM((CHUNKS, MEM, CELLS), F32),
            pltpu.VMEM((TURNS, OBS, COLS_DEV), BF16),
            pltpu.VMEM((len(CROSS), OBS, OBS), BF16),
            pltpu.VMEM((TURNS, MEM, OBS), F32),
            pltpu.VMEM((TURNS, OBS, 3 * MEM), BF16),
            pltpu.VMEM((TURNS, 2 * MEM, OBS), BF16),
            *[pltpu.VMEM((rows, LANES), F32) for rows in (A_ROWS, A_ROWS, B_ROWS, B_ROWS, D_ROWS, D_ROWS)],
            *room(A_ROWS, True), *room(B_ROWS, True), *room(D_ROWS, False),
            pltpu.VMEM((X_ROWS, OBS), F32), pltpu.VMEM((2, 4, X_ROWS, OBS), F32), pltpu.VMEM((X_ROWS, OBS), F32),
            pltpu.VMEM((2, 3, X_ROWS // 2, OBS), F32), pltpu.VMEM((2, 3, X_ROWS // 2, OBS), F32),
            dma((CHUNKS, 3)), dma((CHUNKS, 3)), dma((CHUNKS,)),
            dma((CHUNKS, 3)), dma((CHUNKS, 3)), dma((CHUNKS,)),
            dma((4,)), dma((5, 2, 3)), dma((5, 2, 3)),
            dma((4,)), dma((5, 2, 3)), dma((5, 2, 3)),
            dma((4,)), dma((5, 2, 3)), dma((5, 2, 3)),
            dma((4,)), dma((3, 2, 3)), dma((3, 2, 3)),
            dma((6,)), dma((4,)),
        ],
        compiler_params=pltpu.CompilerParams(
            collective_id=0, has_side_effects=True, vmem_limit_bytes=60 << 20),
        name="filter",
    )(batch_order, owner_region, obs_cell, obs_value, obs_var, loc_weight, flat)
    return out.reshape(SLAB, STACK, COLS_REG)


def solution(mesh):
    return jax.shard_map(
        body,
        mesh=mesh,
        in_specs=(P("grp", None, "region"), P(None, ("region", "grp"), None), P(), P(), P(), P(), P()),
        out_specs=P("grp", None, "region"),
        check_vma=False,
    )
```

```python
import functools

import jax
import jax.numpy as jnp
from jax import lax
from jax.experimental import pallas as pl
from jax.experimental.pallas import tpu as pltpu
from jax.sharding import PartitionSpec as P

epsilon = 1e-05
MESH = pl.DeviceIdType.MESH
F32, BF16 = jnp.float32, jnp.bfloat16

TURNS, OBS, MEM, SLAB, STACK = 8, 256, 80, 20, 16
COLS_REG, COLS_DEV = 2048, 512
GROUP = 4
LANES = 128
FIRST = [(a, b) for b in range(GROUP) for a in range(b)]
SECOND = [(a, b) for b in range(GROUP, TURNS) for a in range(GROUP, b)]
CROSS = [(a, b) for b in range(GROUP, TURNS) for a in range(GROUP)]
FIRST_ROW = {p: i * OBS for i, p in enumerate(FIRST)}
SECOND_ROW = {p: i * OBS for i, p in enumerate(SECOND)}
CROSS_AT = {p: i for i, p in enumerate(CROSS)}
A_ROWS = 2 * len(FIRST) * OBS
B_ROWS = 2 * len(SECOND) * OBS
D_USED = 2 * (TURNS - GROUP) * MEM
D_ROWS = -(-D_USED // 128) * 128
X_ROWS = TURNS * 24 // 2
PIECES = 2
CHUNKS, CHUNK = 4, 128
CELLS = STACK * CHUNK
EARLY = [GROUP, GROUP - 1, GROUP - 1, GROUP - 1]


def split2(value):
    high = value.astype(BF16)
    low = (value - high.astype(F32)).astype(BF16)
    return high, low


def increment(x, left, change, weights):
    anom = x - jnp.sum(x, 0, keepdims=True) * (1.0 / MEM)
    high, low = split2(anom)
    stacked = jnp.concatenate([high, high, low], 0)
    gain = jnp.dot(left, stacked, preferred_element_type=F32) * weights
    g_high, g_low = split2(gain)
    first = jnp.dot(change, g_high, preferred_element_type=F32)
    second = jnp.dot(change[:MEM], g_low, preferred_element_type=F32)
    return first[:MEM] + first[MEM:] + second


def turn_operands(prior, value, variance):
    centre = jnp.sum(prior, 0, keepdims=True) * (1.0 / MEM)
    anom = prior - centre
    spread = jnp.sum(anom * anom, 0, keepdims=True) / (MEM - 1) + epsilon
    denom = spread + variance
    post = (variance * centre + spread * value) / denom
    factor = jnp.sqrt(variance / denom)
    change = post + factor * anom - prior
    scaled = anom * (1.0 / ((MEM - 1) * spread))
    high = scaled.astype(BF16).astype(F32)
    low = scaled - high
    left = jnp.concatenate([high, low, high], 0).T.astype(BF16)
    c_high, c_low = split2(change)
    return left, jnp.concatenate([c_high, c_low], 0)


def places():
    region, z = lax.axis_index("region"), lax.axis_index("grp")
    return region // 8, (region // 2) % 4, region % 2, z


def peer(axis, k):
    x, y, c, z = places()
    if axis == "x":
        x = lax.rem(x + k, 4)
    elif axis == "y":
        y = lax.rem(y + k, 4)
    elif axis == "z":
        z = lax.rem(z + k, 4)
    else:
        c = 1 - c
    return (x * 8 + y * 2 + c, z)


def remote(src, dst, send, recv, device):
    return pltpu.make_async_remote_copy(src, dst, send, recv, device_id=device, device_id_type=MESH)


def started(copies):
    for copy in copies:
        copy.start()
    return copies


def wait(copies):
    for copy in copies:
        copy.wait()


def swap_halves(src, dst, sems, k):
    return started([remote(src, dst, sems.at[2 * k], sems.at[2 * k + 1], peer("c", 1))])


def all_sum(a, b, rows, twice, sib, in0, in1, in2, sib_sem, send, recv):
    x, y, c, z = places()
    at = {"x": x, "y": y}
    orders = (("x", "y"), ("y", "x"))
    h = rows // 2
    t = h // 2
    q = t // 4
    r = q // 4 if twice else q
    base, other = pl.multiple_of(c * h, 8), pl.multiple_of((1 - c) * h, 8)
    block = [pl.multiple_of(base + i * t, 8) for i in range(2)]
    quarter = [pl.multiple_of(block[i] + at[orders[i][0]] * q, 8) for i in range(2)]
    own = quarter
    if twice:
        own = [pl.multiple_of(quarter[i] + at[orders[i][1]] * r, 8) for i in range(2)]

    copies = swap_halves(a.at[pl.ds(other, h)], sib, sib_sem, 0)
    yield
    wait(copies)
    a[pl.ds(base, h), :] += sib[...]

    def exchange(phase, pick, inbox, axis_of):
        return started([
            remote(a.at[pl.ds(pick(i, k), inbox.shape[2])], inbox.at[i, k - 1], send.at[phase, i, k - 1],
                   recv.at[phase, i, k - 1], peer(axis_of(i), k))
            for k in (1, 2, 3) for i in range(2)])

    def added(i, at, inbox):
        return a[pl.ds(at, inbox.shape[2]), :] + inbox[i, 0] + inbox[i, 1] + inbox[i, 2]

    copies = exchange(0, lambda i, k: pl.multiple_of(block[i] + lax.rem(at[orders[i][0]] + k, 4) * q, 8),
                      in0, lambda i: orders[i][0])
    yield
    wait(copies)
    for i in range(2):
        a[pl.ds(quarter[i], q), :] = added(i, quarter[i], in0)

    def second(i, k):
        if twice:
            return pl.multiple_of(quarter[i] + lax.rem(at[orders[i][1]] + k, 4) * r, 8)
        return quarter[i]

    copies = exchange(1, second, in1, lambda i: orders[i][1])
    yield
    wait(copies)
    for i in range(2):
        a[pl.ds(own[i], r), :] = added(i, own[i], in1)
    copies = exchange(2, lambda i, k: own[i], in2, lambda i: "z")
    yield
    wait(copies)
    for i in range(2):
        b[pl.ds(own[i], r), :] = added(i, own[i], in2)

    def gather(phase, place, size, axis_of):
        return started([
            remote(b.at[pl.ds(place[i], size)], b.at[pl.ds(place[i], size)], send.at[phase, i, k - 1],
                   recv.at[phase, i, k - 1], peer(axis_of(i), k))
            for k in (1, 2, 3) for i in range(2)])

    if twice:
        copies = gather(3, own, r, lambda i: orders[i][1])
        yield
        wait(copies)
    copies = gather(4, quarter, q, lambda i: orders[i][0])
    yield
    wait(copies)
    half = b.at[pl.ds(base, h)]
    copies = swap_halves(half, half, sib_sem, 1)
    yield
    wait(copies)


def prior_sum(mine, half, all_of, sib, in0, in1, sib_sem, send, recv):
    x, y, c, z = places()
    orders = (("x", "y"), ("y", "x"))
    t = X_ROWS // 2
    base, other = pl.multiple_of(c * X_ROWS, 8), pl.multiple_of((1 - c) * X_ROWS, 8)

    copies = swap_halves(mine.at[pl.ds(other, X_ROWS)], sib, sib_sem, 0)
    yield
    wait(copies)
    half[...] = mine[pl.ds(base, X_ROWS), :] + sib[...]
    for phase, inbox in enumerate((in0, in1)):
        copies = started([
            remote(half.at[i * t:(i + 1) * t], inbox.at[i, k - 1], send.at[phase, i, k - 1], recv.at[phase, i, k - 1],
                   peer(orders[i][phase], k))
            for k in (1, 2, 3) for i in range(2)])
        yield
        wait(copies)
        for i in range(2):
            value = half[i * t:(i + 1) * t, :] + inbox[i, 0] + inbox[i, 1] + inbox[i, 2]
            if phase == 0:
                half[i * t:(i + 1) * t, :] = value
            else:
                all_of[c, z, i * t:(i + 1) * t, :] = value
    spot = all_of.at[c, z]
    copies = started([remote(spot, spot, send.at[2, 0, k - 1], recv.at[2, 0, k - 1], peer("z", k)) for k in (1, 2, 3)])
    yield
    wait(copies)
    spot = all_of.at[c]
    copies = swap_halves(spot, spot, sib_sem, 1)
    yield
    wait(copies)


def main_kernel(order_in, owner_in, cells_in, values_in, variances_in, weights_in, ens, out,
                order, owner, cells, values, variances, weights, held, pieces, picked,
                stage, outbox, state, wt, cross, prior, left, change,
                a, a_sum, b, b_sum, d, d_sum, *rest):
    (sib_a, in0_a, in1_a, in2_a, sib_b, in0_b, in1_b, in2_b, sib_d, in0_d, in1_d, in2_d, x_half, x_all, sib_x, in0_x, in1_x,
     go_send, go_recv, go_own, back_send, back_recv, back_own,
     sibsem_a, send_a, recv_a, sibsem_b, send_b, recv_b, sibsem_d, send_d, recv_d,
     sibsem_x, send_x, recv_x, in_sems, held_sems) = rest
    region, z = lax.axis_index("region"), lax.axis_index("grp")

    barrier = pltpu.get_barrier_semaphore()
    around = [peer(axis, k) for axis in ("x", "y", "z") for k in (1, 2, 3)] + [peer("c", 1)]
    for device in around:
        pl.semaphore_signal(barrier, 1, device_id=device, device_id_type=MESH)

    arrays = ((order_in, order), (owner_in, owner), (cells_in, cells), (weights_in, weights),
              (values_in, values), (variances_in, variances))
    loads = started([pltpu.make_async_copy(src, dst, in_sems.at[i]) for i, (src, dst) in enumerate(arrays)])
    blocks = started([
        pltpu.make_async_copy(ens.at[:, k * COLS_DEV:(k + 1) * COLS_DEV], held.at[k], held_sems.at[k]) for k in range(4)])
    wait(loads)

    def go(q):
        here = pl.ds(pl.multiple_of(z * COLS_DEV + q * CHUNK, 128), CHUNK)
        copies = [pltpu.make_async_copy(ens.at[:, here], stage.at[z, q], go_own.at[q])]
        for k in (1, 2, 3):
            there = pl.ds(pl.multiple_of(lax.rem(z + k, 4) * COLS_DEV + q * CHUNK, 128), CHUNK)
            copies.append(remote(ens.at[:, there], stage.at[z, q], go_send.at[q, k - 1], go_recv.at[q, k - 1],
                                 peer("z", k)))
        return started(copies)

    def back(q):
        there = pl.ds(pl.multiple_of(z * COLS_DEV + q * CHUNK, 128), CHUNK)
        copies = [pltpu.make_async_copy(outbox.at[z, q], out.at[:, there], back_own.at[q])]
        for k in (1, 2, 3):
            copies.append(remote(outbox.at[lax.rem(z + k, 4), q], out.at[:, there],
                                 back_send.at[q, k - 1], back_recv.at[q, k - 1], peer("z", k)))
        return copies

    def turned(t):
        wt[t] = weights[order[t]].T

    def select(n):
        column = cells[pl.ds(order[n], 1), :] & (COLS_REG - 1)
        local = jnp.where(owner[order[n]] == region, column - z * COLS_DEV, -1)
        return jnp.where(lax.broadcasted_iota(jnp.int32, (COLS_DEV, OBS), 0) == local, 1.0, 0.0).astype(BF16)

    def at_columns(t, chosen):
        return jnp.dot(wt[t], chosen, preferred_element_type=F32)

    def put_pair(buffer, rows, row, value):
        buffer[row:row + OBS, :] = value[:, :LANES]
        buffer[rows // 2 + row:rows // 2 + row + OBS, :] = value[:, LANES:]

    def get_pair(buffer, rows, row):
        return jnp.concatenate([buffer[row:row + OBS, :], buffer[rows // 2 + row:rows // 2 + row + OBS, :]], 1)

    for t in range(GROUP - 1):
        turned(t)
    for n in range(1, GROUP):
        chosen = select(n)
        for t in range(n):
            put_pair(a, A_ROWS, FIRST_ROW[t, n], at_columns(t, chosen))

    sum_x = prior_sum(picked, x_half, x_all, sib_x, in0_x, in1_x, sibsem_x, send_x, recv_x)
    sum_a = all_sum(a, a_sum, A_ROWS, True, sib_a, in0_a, in1_a, in2_a, sibsem_a, send_a, recv_a)
    sum_b = all_sum(b, b_sum, B_ROWS, True, sib_b, in0_b, in1_b, in2_b, sibsem_b, send_b, recv_b)
    sum_d = all_sum(d, d_sum, D_ROWS, False, sib_d, in0_d, in1_d, in2_d, sibsem_d, send_d, recv_d)

    def pick(n, _):
        cell = cells[pl.ds(order[n], 1), :]
        column = jnp.where(owner[order[n]] == region, cell & (COLS_REG - 1), -1)
        total = jnp.zeros((SLAB * STACK, OBS), F32)
        for k in range(4):
            rows = lax.broadcasted_iota(jnp.int32, (COLS_DEV, OBS), 0) + k * COLS_DEV
            chosen = jnp.where(rows == column, 1.0, 0.0).astype(BF16)
            got = jnp.dot(pieces[k], chosen, preferred_element_type=F32)
            for i in range(PIECES):
                total = total + got[i * SLAB * STACK:(i + 1) * SLAB * STACK]
        levels = lax.broadcasted_iota(jnp.int32, (SLAB, STACK, OBS), 1)
        value = jnp.where(levels == (cell >> 11)[None], total.reshape(SLAB, STACK, OBS), 0.0)
        picked[pl.ds(pl.multiple_of(n * 24, 8), SLAB), :] = jnp.sum(value, 1)
        return 0

    pl.semaphore_wait(barrier, len(around))
    next(sum_a)
    sent = [go(0), go(1)]
    picked[...] = jnp.zeros_like(picked)
    for k in range(4):
        wait(blocks[k:k + 1])
        rest_of = held[k]
        for i in range(PIECES):
            piece = rest_of.astype(BF16)
            pieces[k, i * SLAB * STACK:(i + 1) * SLAB * STACK, :] = piece
            rest_of = rest_of - piece.astype(F32)
    next(sum_a)
    lax.fori_loop(0, 6, pick, 0)
    next(sum_a)
    lax.fori_loop(6, TURNS, pick, 0)
    next(sum_x)
    for t in range(GROUP - 1, TURNS):
        turned(t)
    next(sum_x)
    next(sum_a)
    for n in range(GROUP + 1, TURNS):
        chosen = select(n)
        for t in range(GROUP, n):
            put_pair(b, B_ROWS, SECOND_ROW[t, n], at_columns(t, chosen))
    next(sum_b)
    next(sum_x)
    next(sum_a)
    next(sum_b)
    next(sum_x)
    next(sum_a)
    for n in range(GROUP, TURNS):
        chosen = select(n)
        for t in range(GROUP):
            cross[CROSS_AT[t, n]] = at_columns(t, chosen).astype(BF16)
    d[...] = jnp.zeros_like(d)
    next(sum_x)
    sent += [go(2)]
    next(sum_b)
    next(sum_a)
    next(sum_b)
    next(sum_x, None)
    next(sum_a, None)

    def assimilate(t):
        left[t], change[t] = turn_operands(
            prior[t], values[pl.ds(order[t], 1), :], variances[pl.ds(order[t], 1), :])

    def first_prior(n):
        at = (n % 4) * 24
        for k in range(4):
            prior[n, k * SLAB:(k + 1) * SLAB, :] = x_all[n // 4, k, at:at + SLAB, :]

    for n in range(TURNS):
        first_prior(n)
    for t in range(GROUP):
        assimilate(t)
        for n in range(t + 1, TURNS):
            if n < GROUP:
                prior[n] += increment(prior[n], left[t], change[t], get_pair(a_sum, A_ROWS, FIRST_ROW[t, n]))
            else:
                at = (n - GROUP) * 2 * MEM
                step = increment(prior[n], left[t], change[t], cross[CROSS_AT[t, n]].astype(F32))
                d[at:at + MEM, :] += step[:, :LANES]
                d[at + MEM:at + 2 * MEM, :] += step[:, LANES:]
                prior[n] += step
    next(sum_d)

    def turn(q, t):
        lanes = pl.ds(pl.multiple_of(q * CHUNK, 128), CHUNK)
        w_t = jnp.concatenate([wt[t, :, lanes].astype(F32)] * STACK, 1)
        x = state[q]
        state[q] = x + increment(x, left[t], change[t], w_t)

    def turns(q, first, last):
        def one(t, _):
            turn(q, t)
            return 0

        lax.fori_loop(first, last, one, 0)

    def early(q):
        def level(s, _):
            lanes = pl.ds(pl.multiple_of(s * CHUNK, 128), CHUNK)
            for k in range(4):
                state[q, k * SLAB:(k + 1) * SLAB, lanes] = stage[k, q, pl.ds(s, SLAB, stride=STACK), :]
            return 0

        lax.fori_loop(0, STACK, level, 0)
        turns(q, 0, EARLY[q])

    next(sum_d)
    next(sum_b)
    sent += [go(3)]
    wait(sent[0])
    early(0)
    next(sum_d)
    wait(sent[1])
    early(1)
    next(sum_b)
    next(sum_d)
    wait(sent[2])
    early(2)
    next(sum_d)
    next(sum_b)
    wait(sent[3])
    early(3)
    next(sum_d)
    next(sum_d, None)

    for n in range(GROUP, TURNS):
        first_prior(n)
        at = (n - GROUP) * 2 * MEM
        prior[n] += jnp.concatenate([d_sum[at:at + MEM, :], d_sum[at + MEM:at + 2 * MEM, :]], 1)
    for t in range(GROUP, TURNS):
        assimilate(t)
        if t == GROUP:
            next(sum_b, None)
        for n in range(t + 1, TURNS):
            prior[n] += increment(prior[n], left[t], change[t], get_pair(b_sum, B_ROWS, SECOND_ROW[t, n]))
        turn(0, t)

    def give(q):
        def level(s, _):
            lanes = pl.ds(pl.multiple_of(s * CHUNK, 128), CHUNK)
            for k in range(4):
                outbox[k, q, pl.ds(s, SLAB, stride=STACK), :] = state[q, k * SLAB:(k + 1) * SLAB, lanes]
            return 0

        lax.fori_loop(0, STACK, level, 0)
        started(back(q))

    def late(q, _):
        turns(q, EARLY[1], TURNS)
        give(q)
        return 0

    give(0)
    lax.fori_loop(1, CHUNKS, late, 0)
    for q in range(CHUNKS):
        wait(back(q))


def body(ensemble, loc_weight, obs_value, obs_var, owner_region, obs_cell, batch_order):
    flat = ensemble.reshape(SLAB * STACK, COLS_REG)
    dma = pltpu.SemaphoreType.DMA

    def room(rows, twice):
        return [pltpu.VMEM((rows // 2, LANES), F32)] + [
            pltpu.VMEM((2, 3, rows // cut, LANES), F32) for cut in ((16, 64, 64) if twice else (16, 16, 16))]

    out = pl.pallas_call(
        main_kernel,
        out_shape=jax.ShapeDtypeStruct((SLAB * STACK, COLS_REG), F32),
        in_specs=[pl.BlockSpec(memory_space=pltpu.HBM)] * 7,
        out_specs=pl.BlockSpec(memory_space=pl.ANY),
        scratch_shapes=[
            pltpu.SMEM((TURNS,), jnp.int32), pltpu.SMEM((TURNS,), jnp.int32), pltpu.VMEM((TURNS, OBS), jnp.int32),
            pltpu.VMEM((TURNS, OBS), F32), pltpu.VMEM((TURNS, OBS), F32),
            pltpu.VMEM((TURNS, COLS_DEV, OBS), BF16),
            pltpu.VMEM((4, SLAB * STACK, COLS_DEV), F32),
            pltpu.VMEM((4, PIECES * SLAB * STACK, COLS_DEV), BF16),
            pltpu.VMEM((TURNS * 24, OBS), F32),
            pltpu.VMEM((4, CHUNKS, SLAB * STACK, CHUNK), F32),
            pltpu.VMEM((4, CHUNKS, SLAB * STACK, CHUNK), F32),
            pltpu.VMEM((CHUNKS, MEM, CELLS), F32),
            pltpu.VMEM((TURNS, OBS, COLS_DEV), BF16),
            pltpu.VMEM((len(CROSS), OBS, OBS), BF16),
            pltpu.VMEM((TURNS, MEM, OBS), F32),
            pltpu.VMEM((TURNS, OBS, 3 * MEM), BF16),
            pltpu.VMEM((TURNS, 2 * MEM, OBS), BF16),
            *[pltpu.VMEM((rows, LANES), F32) for rows in (A_ROWS, A_ROWS, B_ROWS, B_ROWS, D_ROWS, D_ROWS)],
            *room(A_ROWS, True), *room(B_ROWS, True), *room(D_ROWS, False),
            pltpu.VMEM((X_ROWS, OBS), F32), pltpu.VMEM((2, 4, X_ROWS, OBS), F32), pltpu.VMEM((X_ROWS, OBS), F32),
            pltpu.VMEM((2, 3, X_ROWS // 2, OBS), F32), pltpu.VMEM((2, 3, X_ROWS // 2, OBS), F32),
            dma((CHUNKS, 3)), dma((CHUNKS, 3)), dma((CHUNKS,)),
            dma((CHUNKS, 3)), dma((CHUNKS, 3)), dma((CHUNKS,)),
            dma((4,)), dma((5, 2, 3)), dma((5, 2, 3)),
            dma((4,)), dma((5, 2, 3)), dma((5, 2, 3)),
            dma((4,)), dma((5, 2, 3)), dma((5, 2, 3)),
            dma((4,)), dma((3, 2, 3)), dma((3, 2, 3)),
            dma((6,)), dma((4,)),
        ],
        compiler_params=pltpu.CompilerParams(
            collective_id=0, has_side_effects=True, vmem_limit_bytes=60 << 20),
        name="filter",
    )(batch_order, owner_region, obs_cell, obs_value, obs_var, loc_weight, flat)
    return out.reshape(SLAB, STACK, COLS_REG)


def solution(mesh):
    return jax.shard_map(
        body,
        mesh=mesh,
        in_specs=(P("grp", None, "region"), P(None, ("region", "grp"), None), P(), P(), P(), P(), P()),
        out_specs=P("grp", None, "region"),
        check_vma=False,
    )
```
